32 devices in a mesh: ctx: 8 (over z, core), exp: 4 (over y, x).
Axes of the slice: x: 2, y: 2, z: 4, core: 2. Of those that a mesh axis runs over, the one named last changes fastest.
Arguments:
- queries: bfloat16 [768, 6144], P('ctx', 'exp'), may hold values from -10 to 10
- rotated_keys: bfloat16 [768, 1024], P('ctx', 'exp'), may hold values from -10 to 10
- values: bfloat16 [768, 1024], P('ctx', 'exp'), may hold values from -6 to 6
- residual: bfloat16 [768, 6144], P('ctx', 'exp'), may hold values from -45 to 45
- span_order: int32 [8], replicated, may hold values from 0 to 7, each once
- norm_gain: bfloat16 [6144], replicated, may hold values from 0.25 to 1.75
- router_weight: bfloat16 [6144, 4], replicated, may hold values from -0.078125 to 0.078125
- expert_ids: int32 [768, 2], P(('ctx', 'exp')), may hold values from 0 to 3, all different within a row; in each aligned block of 24 rows (0 to 23, 24 to 47, ...) at most 18 rows name the same one
- gate_weight: bfloat16 [4, 6144, 8192], P('exp', None, 'ctx'), may hold values from -0.078125 to 0.078125
- up_weight: bfloat16 [4, 6144, 8192], P('exp', None, 'ctx'), may hold values from -0.078125 to 0.078125
- down_weight: bfloat16 [4, 8192, 6144], P('exp', 'ctx'), may hold values from -0.0625 to 0.0625
Outputs:
- layer_out: bfloat16 [768, 6144], P('ctx', 'exp')
The draws below stay inside these ranges and needn't reach their ends.
Inputs may be any that keep to these rules, and one draw needn't show every extreme that they name: `expert_ids`: each row names two different experts. In each aligned block of 24 rows, no expert is named by more than 18 rows, a bound that some block reaches.
All inputs are finite; a program needn't handle non-finite values.
Results may differ from the reference program's by a relative error of at most 0.012.
Values may be sent and summed in bfloat16 or wider, within the bound.
No kernel may reach another device: no remote copies, remote signals or barrier semaphores. Data moves between devices by JAX's collectives and lax.ppermute only.
A program may use at most 128 MiB of HBM per device.

```python
import math
import jax
import jax.numpy as jnp
import numpy as np
from jax import lax

D = 6144
QUERY_HEADS = 48
KEY_VALUE_HEADS = 8
HEAD_WIDTH = 128
EXPERTS = 4
FF_WIN = 8192
TOP = 2
TOK_CTX = 96
TOK_SUB = 24
SEQUENCE_TOKENS = 768
CAP = 18
N_CTX = 8


def pair_draw(key):
    query_part = jnp.clip(1.4 * jax.random.normal(jax.random.fold_in(key, 101), (SEQUENCE_TOKENS, QUERY_HEADS * HEAD_WIDTH), jnp.float32), -6.0, 6.0)
    key_portion = jnp.clip(1.4 * jax.random.normal(jax.random.fold_in(key, 102), (SEQUENCE_TOKENS, KEY_VALUE_HEADS * HEAD_WIDTH), jnp.float32), -6.0, 6.0)
    return (query_part, key_portion)


def draw_queries(key, part):
    return pair_draw(key)[0].astype(jnp.bfloat16)


def draw_rotated_keys(key, part):
    return pair_draw(key)[1].astype(jnp.bfloat16)


def draw_residual(key, part):
    base_draw = jnp.clip(jax.random.normal(jax.random.fold_in(key, 201), (SEQUENCE_TOKENS, D), jnp.float32), -4.0, 4.0)
    return base_draw.astype(jnp.bfloat16)


def shard_levels(own_key, shape, split, low, top_value):
    def one(dim, shards_of):
        draws = jax.random.uniform(jax.random.fold_in(jax.random.fold_in(own_key, 6), dim), (shards_of,), jnp.float32, low / len(split), top_value / len(split))
        return jnp.repeat(jnp.exp(draws), shape[dim] // shards_of).reshape((-1,) + (1,) * (len(shape) - dim - 1))

    gain = one(*split[0])
    for cut in split[1:]:
        gain = gain * one(*cut)
    return gain


def assign_block(own_key, own, number, rows, number_of, top, reach, slope):
    sequence = jax.random.permutation(own_key, number_of)
    crowded, common = load_shares(number_of, rows * top, reach, slope, True), load_shares(number_of, rows * top, reach, slope, False)
    places = jnp.arange(number_of)

    def named(lengths, rotation):
        used = int((lengths > 0).sum())
        fixed = max(1, used // 4)
        passed = fixed + (places - fixed + rotation * (used - fixed)) % max(1, number_of - fixed)
        return jnp.zeros((number_of,), jnp.int32).at[sequence[jnp.where(places < fixed, places, passed)]].set(jnp.asarray(lengths, jnp.int32))

    lengths = jnp.where(number % 4 == 0, named(crowded, number // 4), named(common, number - number // 4 - 1))
    mixed = jax.random.permutation(jax.random.fold_in(own, 3), number_of)
    source_of, taker = mixed[0:number_of // 2 * 2:2], mixed[1:number_of // 2 * 2:2]
    margin = jnp.minimum(lengths[source_of] - 1, reach - lengths[taker]) // 2
    margin = jnp.where((source_of == sequence[0]) | (taker == sequence[0]) | (lengths[taker] == 0), 0, jnp.maximum(margin, 0))
    passed = jax.random.randint(jax.random.fold_in(own, 4), (number_of // 2,), 0, 1 << 20) % (margin + 1)
    lengths = lengths.at[source_of].add(-passed).at[taker].add(passed)
    labels = jnp.searchsorted(jnp.cumsum(lengths), jnp.arange(rows * top), side="right").astype(jnp.int32)
    grid = labels.reshape(top, rows).T
    grid = grid[jax.random.permutation(jax.random.fold_in(own, 1), rows)]
    rotation = jax.random.randint(jax.random.fold_in(own, 2), (rows, 1), 0, top)
    return jnp.take_along_axis(grid, (jnp.arange(top)[None, :] + rotation) % top, axis=1)


def load_shares(count, total, limit, slope, full):
    weights = [(1 << 20) // math.isqrt(grade ** slope) + 1 for grade in range(1, count + 1)]
    largest = limit if full else min(limit, max(-(-total // count), total * weights[0] // sum(weights)))
    least = 1 if total - largest >= count - 1 else 0
    holding, surplus = [largest] + [least] * (count - 1), total - largest - least * (count - 1)
    while surplus > 0:
        free = [i for i in range(1, count) if holding[i] < largest] or [i for i in range(1, count) if holding[i] < limit]
        pool, remaining = sum([weights[i] for i in free]), surplus
        for i in free:
            addition = min(limit - holding[i], max(1, remaining * weights[i] // pool), surplus)
            holding[i] = holding[i] + addition
            surplus = surplus - addition
    return np.array(holding)


def gaussian(rng, extent, spread, bound, cuts=(), kind=jnp.bfloat16):
    result = spread * jax.random.normal(rng, extent, jnp.float32)
    if cuts:
        result = result * shard_levels(rng, extent, cuts, -0.22, 0.18)
    return jnp.clip(result, -bound, bound).astype(kind)


def setup_inputs(seed: int = 0) -> dict:
    arg_keys = jax.random.split(jax.random.key(seed), 12)
    queries = draw_queries(jax.random.fold_in(arg_keys[11], 71), 0)
    rotated_keys = draw_rotated_keys(jax.random.fold_in(arg_keys[11], 71), 0)
    values = gaussian(arg_keys[2], (SEQUENCE_TOKENS, KEY_VALUE_HEADS * HEAD_WIDTH), 1.0, 6.0, ((0, 8), (1, 4)))
    residual = draw_residual(jax.random.fold_in(arg_keys[11], 71), 0)
    span_order = jax.random.permutation(arg_keys[4], N_CTX).astype(jnp.int32)
    norm_gain = jnp.clip(1.0 + 0.15 * jax.random.normal(arg_keys[5], (D,), jnp.float32), 0.25, 1.75).astype(jnp.bfloat16)
    router_weight = gaussian(arg_keys[6], (D, EXPERTS), D ** -0.5, 0.078125)
    expert_ids_keys = jax.random.split(jax.random.fold_in(arg_keys[7], 1), SEQUENCE_TOKENS // TOK_SUB)
    expert_ids_turns = jax.random.permutation(jax.random.fold_in(arg_keys[7], 3), SEQUENCE_TOKENS // TOK_SUB)
    expert_ids = jax.vmap(lambda own, number: assign_block(jax.random.fold_in(arg_keys[7], 2), own, number, TOK_SUB, EXPERTS, TOP, CAP, 2))(expert_ids_keys, expert_ids_turns).reshape((SEQUENCE_TOKENS, TOP))
    gate_weight = gaussian(arg_keys[8], (EXPERTS, D, FF_WIN), D ** -0.5, 0.078125, ((0, 4), (2, 8)))
    up_weight = gaussian(arg_keys[9], (EXPERTS, D, FF_WIN), D ** -0.5, 0.078125, ((0, 4), (2, 8)))
    down_weight = gaussian(arg_keys[10], (EXPERTS, FF_WIN, D), FF_WIN ** -0.5, 0.0625, ((0, 4), (1, 8)))
    return dict(queries=queries, rotated_keys=rotated_keys, values=values, residual=residual, span_order=span_order, norm_gain=norm_gain, router_weight=router_weight, expert_ids=expert_ids, gate_weight=gate_weight, up_weight=up_weight, down_weight=down_weight)


def slot_tables(id_pairs, n_experts, capacity):
    width_a = id_pairs.shape[-2] * id_pairs.shape[-1]
    flat_ids = id_pairs.reshape(id_pairs.shape[:-2] + (width_a,))
    expert_hot = (flat_ids[..., None] == jnp.arange(n_experts, dtype=jnp.int32)).astype(jnp.int32)
    earlier = jnp.cumsum(expert_hot, axis=-2) - expert_hot
    slot_index = lax.optimization_barrier(jnp.sum(earlier * expert_hot, axis=-1))
    slot_hot = (slot_index[..., None] == jnp.arange(capacity, dtype=jnp.int32)).astype(jnp.float32)
    slot_table = expert_hot.astype(jnp.float32)[..., :, :, None] * slot_hot[..., :, None, :]
    return jnp.moveaxis(slot_table, -3, -1)

def reference(queries, rotated_keys, values, residual, span_order, norm_gain, router_weight, expert_ids, gate_weight, up_weight, down_weight):
    query_group_width = QUERY_HEADS // KEY_VALUE_HEADS
    row_ids = jnp.arange(SEQUENCE_TOKENS, dtype=jnp.int32)
    positions = span_order[row_ids // TOK_CTX] * TOK_CTX + row_ids % TOK_CTX
    visible = positions[None, :] <= positions[:, None]
    logit_scale_factor = 1.0 / math.sqrt(HEAD_WIDTH)
    query_head_rows = queries.reshape(SEQUENCE_TOKENS, KEY_VALUE_HEADS, query_group_width, HEAD_WIDTH).transpose(1, 0, 2, 3)
    key_head_rows = rotated_keys.reshape(SEQUENCE_TOKENS, KEY_VALUE_HEADS, HEAD_WIDTH).transpose(1, 0, 2)
    value_head_rows = values.reshape(SEQUENCE_TOKENS, KEY_VALUE_HEADS, HEAD_WIDTH).transpose(1, 0, 2)

    def per_head(operands):
        single_query, single_key, single_value = operands
        attention_logits = jnp.einsum('fls,xs->lfx', single_query.astype(jnp.float32), single_key.astype(jnp.float32)) * logit_scale_factor
        masked = jnp.where(visible[None], attention_logits, -jnp.inf)
        peak = lax.optimization_barrier(jnp.max(masked, axis=-1, keepdims=True))
        weights = jnp.where(visible[None], jnp.exp(attention_logits - peak), 0.0)
        totals = lax.optimization_barrier(jnp.sum(weights, axis=-1))
        attention_weights = lax.optimization_barrier(weights.astype(jnp.bfloat16))
        blended_output = jnp.einsum('njc,cs->jns', attention_weights.astype(jnp.float32), single_value.astype(jnp.float32))
        return blended_output / jnp.transpose(totals)[:, :, None]
    attended = lax.map(per_head, (query_head_rows, key_head_rows, value_head_rows))
    attended = attended.transpose(1, 0, 2, 3).reshape(SEQUENCE_TOKENS, D)
    hidden = (residual.astype(jnp.float32) + attended).astype(jnp.bfloat16)
    hidden_f = hidden.astype(jnp.float32)
    mean_sq = lax.optimization_barrier(jnp.mean(hidden_f * hidden_f, axis=-1, keepdims=True))
    normed = (hidden_f * lax.rsqrt(mean_sq + 1e-05) * norm_gain.astype(jnp.float32)).astype(jnp.bfloat16)
    logits = jnp.dot(normed, router_weight, preferred_element_type=jnp.float32)
    id_hot = (expert_ids[..., None] == jnp.arange(EXPERTS, dtype=jnp.int32)).astype(jnp.float32)
    chosen = lax.optimization_barrier(jnp.sum(logits[:, None, :] * id_hot, axis=-1))
    mix_weight = jax.nn.sigmoid(chosen - chosen[:, ::-1])
    blocks = SEQUENCE_TOKENS // TOK_SUB
    slot_table = slot_tables(expert_ids.reshape(blocks, TOK_SUB, 2), EXPERTS, CAP)
    token_table = lax.optimization_barrier(jnp.sum(slot_table.reshape(blocks, EXPERTS, CAP, TOK_SUB, 2), axis=-1))
    buffer = jnp.einsum('bect,btd->ebcd', token_table, normed.reshape(blocks, TOK_SUB, D).astype(jnp.float32))
    buffer = buffer.astype(jnp.bfloat16).reshape(EXPERTS, blocks * CAP, D)
    unit_share = FF_WIN // N_CTX

    def per_expert(operands):
        expert_rows, gate_one, up_one, down_one = operands
        gate_val = jnp.dot(expert_rows, gate_one, preferred_element_type=jnp.float32)
        up_val = jnp.dot(expert_rows, up_one, preferred_element_type=jnp.float32)
        activation = (jax.nn.silu(gate_val) * up_val).astype(jnp.bfloat16)
        row_total = activation.shape[0]
        pieces_a = activation.reshape(row_total, N_CTX, unit_share).transpose(1, 0, 2)
        pieces_w = down_one.reshape(N_CTX, unit_share, D)

        def add_share(running, share_pair):
            part_out = lax.optimization_barrier(jnp.dot(share_pair[0], share_pair[1], preferred_element_type=jnp.float32).astype(jnp.bfloat16))
            return (running + part_out.astype(jnp.float32), None)
        summed = lax.scan(add_share, jnp.zeros((row_total, D), jnp.float32), (pieces_a, pieces_w))[0]
        return summed.astype(jnp.bfloat16)
    expert_out = lax.map(per_expert, (buffer, gate_weight, up_weight, down_weight))
    expert_out = expert_out.reshape(EXPERTS, blocks, CAP, D)
    picked = jnp.einsum('beca,ebcd->bad', slot_table, expert_out.astype(jnp.float32)).reshape(SEQUENCE_TOKENS, 2, D)
    layer_out = hidden_f + lax.optimization_barrier(jnp.sum(mix_weight[..., None] * picked, axis=1))
    return layer_out.astype(jnp.bfloat16)
```

```python
import math

import jax
import jax.numpy as jnp
from jax import lax
from jax.sharding import PartitionSpec as P

HEAD_WIDTH = 128
GROUPS = 2


def body(
    queries,
    rotated_keys,
    values,
    residual,
    span_order,
    norm_gain,
    router_weight,
    expert_ids,
    gate_weight,
    up_weight,
    down_weight,
):
    f32, bf16 = jnp.float32, jnp.bfloat16
    tok, width = queries.shape
    n_ctx, n_exp = lax.axis_size("ctx"), lax.axis_size("exp")
    n_chip = n_ctx // 2
    ctx, exp = lax.axis_index("ctx"), lax.axis_index("exp")
    kv_width = rotated_keys.shape[1]
    kv_local = kv_width // HEAD_WIDTH
    group = width // kv_width
    sub = tok // n_exp
    experts = n_exp * gate_weight.shape[0]
    cap = max(2, min(sub, 3 * sub // experts))
    slots = n_exp * cap

    def from_chip(x, d):
        pairs = [(2 * ((i // 2 + d) % n_chip) + i % 2, i) for i in range(n_ctx)]
        return lax.ppermute(x, "ctx", pairs) if d else x

    def from_core(x):
        return lax.ppermute(x, "ctx", [(i ^ 1, i) for i in range(n_ctx)])

    def from_peer(x, k):
        return lax.ppermute(x, "exp", [(i ^ k, i) for i in range(n_exp)]) if k else x

    id_rows = jnp.pad(expert_ids.reshape(-1).astype(bf16), (0, 8 * 2 * kv_width - 2 * sub))
    packed = jnp.concatenate(
        [
            jnp.concatenate([rotated_keys, values], axis=1),
            id_rows.reshape(8, 2 * kv_width),
        ],
        axis=0,
    )
    spans = [from_chip(packed, d) for d in range(n_chip)]
    near = jnp.concatenate([s[:tok] for s in spans], axis=0)
    ids_z = jnp.stack([s[tok:].reshape(-1)[: 2 * sub] for s in spans]).reshape(n_chip, sub, 2)
    far = from_core(near)
    keys_values = jnp.concatenate([near, far], axis=0)
    chip = ctx // 2
    core = ctx % 2
    rel = jnp.arange(n_ctx, dtype=jnp.int32)
    held = 2 * ((chip + rel % n_chip) % n_chip) + jnp.where(rel < n_chip, core, 1 - core)
    all_spans = jnp.arange(n_ctx, dtype=jnp.int32)
    start = jnp.sum(jnp.where(held[:, None] == all_spans[None], span_order[None], 0), axis=1)
    own = jnp.sum(jnp.where(all_spans == ctx, span_order, 0))
    within = jnp.arange(tok, dtype=jnp.int32)
    key_pos = (start[:, None] * tok + within[None]).reshape(-1)
    query_pos = own * tok + within
    visible = key_pos[None, :] <= query_pos[:, None]
    q = queries.reshape(tok, kv_local, group, HEAD_WIDTH)
    k = keys_values[:, :kv_width].reshape(-1, kv_local, HEAD_WIDTH)
    v = keys_values[:, kv_width:].reshape(-1, kv_local, HEAD_WIDTH)
    scores = jnp.einsum("tkgd,skd->kgts", q, k, preferred_element_type=f32) / math.sqrt(HEAD_WIDTH)
    peak = jnp.max(jnp.where(visible, scores, -jnp.inf), axis=-1, keepdims=True)
    weights = jnp.where(visible, jnp.exp(scores - peak), 0.0)
    total = jnp.sum(weights, axis=-1)
    acc = jnp.einsum("kgts,skd->kgtd", weights.astype(bf16), v, preferred_element_type=f32)
    attended = (acc / total[..., None]).transpose(2, 0, 1, 3).reshape(tok, width)
    hidden = (residual.astype(f32) + attended).astype(bf16)

    ids_all = [from_peer(ids_z.astype(f32), k) for k in range(n_exp)]
    ids = jnp.stack([ids_all[0]] + ids_all[1:], axis=1)
    peers = jnp.arange(n_exp, dtype=jnp.int32) ^ exp
    place = (peers[:, None] == jnp.arange(n_exp)[None]).astype(f32)
    ids = jnp.einsum("dksj,kb->dbsj", ids, place, precision=lax.Precision.HIGHEST).reshape(n_chip, tok, 2)
    ids = jnp.round(ids).astype(jnp.int32)
    sent = (ids[:, None, :, :] == peers[None, :, None, None]).any(-1)
    sent_f = sent.astype(f32)
    rank = jnp.cumsum(sent_f, axis=-1) - sent_f
    take = (
        sent[:, :, None, :] & (rank[:, :, None, :] == jnp.arange(slots, dtype=f32)[None, None, :, None])
    ).astype(bf16)

    gate_local, up_local, down_local = gate_weight[0], up_weight[0], down_weight[0]
    gain = norm_gain.astype(f32)
    blocks = [from_chip(hidden, d) for d in range(n_chip)]
    per = n_chip // GROUPS
    merged_parts = [None] * n_chip
    for g in range(GROUPS):
        ds = list(range(g * per, (g + 1) * per))
        picked = [
            jnp.dot(take[d].reshape(n_exp * slots, tok), blocks[d], preferred_element_type=f32)
            .astype(bf16)
            .reshape(n_exp, slots, width)
            for d in ds
        ]
        pieces = [
            from_peer(jnp.concatenate([p[k] for p in picked], axis=0), k) for k in range(n_exp)
        ]
        rows = per * slots
        stacked = pieces
        bit = 1
        while bit < n_exp:
            stacked = [
                jnp.where((exp & bit) != 0, stacked[j ^ bit], stacked[j]) for j in range(n_exp)
            ]
            bit *= 2
        full = jnp.concatenate(stacked, axis=1).astype(f32)
        mean_sq = jnp.mean(full * full, axis=-1, keepdims=True)
        normed = (full * lax.rsqrt(mean_sq + 1e-05) * gain).astype(bf16)
        logits = jnp.dot(normed, router_weight, preferred_element_type=f32)
        take_self = take[ds[0] : ds[-1] + 1, 0]
        row_ids = jnp.einsum(
            "dst,dtj->dsj", take_self.astype(f32), ids[ds[0] : ds[-1] + 1].astype(f32)
        ).reshape(rows, 2)
        own_hot = jnp.arange(experts) == exp
        other = jnp.sum(row_ids, axis=-1) - exp.astype(f32)
        other_hot = jnp.arange(experts, dtype=f32)[None] == other[:, None]
        own_logit = jnp.sum(jnp.where(own_hot[None], logits, 0.0), axis=-1)
        other_logit = jnp.sum(jnp.where(other_hot, logits, 0.0), axis=-1)
        mix = jax.nn.sigmoid(own_logit - other_logit)

        def expert(x):
            gate_val = jnp.dot(x, gate_local, preferred_element_type=f32)
            up_val = jnp.dot(x, up_local, preferred_element_type=f32)
            act = (jax.nn.silu(gate_val) * up_val).astype(bf16)
            return jnp.dot(act, down_local, preferred_element_type=f32)

        far_rows = from_core(normed)
        far_out = expert(far_rows).astype(bf16)
        near_out = expert(normed)
        back = from_core(far_out)
        part = ((near_out + back.astype(f32)) * mix[:, None]).astype(bf16)
        returned = []
        for k in range(n_exp):
            chunk = lax.dynamic_slice_in_dim(part, (exp ^ k) * width, width, axis=1)
            returned.append(from_peer(chunk, k).reshape(per, slots, width))
        for i, d in enumerate(ds):
            table = take[d].reshape(n_exp * slots, tok)
            data = jnp.concatenate([r[i] for r in returned], axis=0)
            merged_parts[d] = lax.dot_general(
                table, data, (((0,), (0,)), ((), ())), preferred_element_type=f32
            )
    total_out = hidden.astype(f32) + merged_parts[0]
    for d in range(1, n_chip):
        total_out += from_chip(merged_parts[d].astype(bf16), n_chip - d).astype(f32)
    return total_out.astype(bf16)


def solution(mesh):
    return jax.shard_map(
        body,
        mesh=mesh,
        in_specs=(
            P("ctx", "exp"),
            P("ctx", "exp"),
            P("ctx", "exp"),
            P("ctx", "exp"),
            P(),
            P(),
            P(),
            P(("ctx", "exp"), None),
            P("exp", None, "ctx"),
            P("exp", None, "ctx"),
            P("exp", "ctx", None),
        ),
        out_specs=P("ctx", "exp"),
        check_vma=False,
    )
```

```python
import functools
import math

import jax
import jax.numpy as jnp
from jax import lax
from jax.experimental import pallas as pl
from jax.experimental.pallas import tpu as pltpu
from jax.sharding import PartitionSpec as P

HEAD_WIDTH = 128
TILE = 16
LANES = 128
F32, BF16 = jnp.float32, jnp.bfloat16
MIB = 2**20
VMEM = pl.BlockSpec(memory_space=pltpu.VMEM)
ANY = pl.BlockSpec(memory_space=pl.ANY)
SMEM = pl.BlockSpec(memory_space=pltpu.SMEM)


def call(kernel, inputs, specs, shapes, limit, scratch=(), flops=0, moved=0, after=()):
    n = len(inputs)

    def ordered(*refs):
        kernel(*refs[:n], *refs[n + len(after) :])

    return pl.pallas_call(
        ordered,
        in_specs=list(specs) + [ANY] * len(after),
        out_specs=[VMEM] * len(shapes),
        out_shape=[jax.ShapeDtypeStruct(s, d) for s, d in shapes],
        scratch_shapes=list(scratch),
        compiler_params=pltpu.CompilerParams(vmem_limit_bytes=limit * MIB),
        cost_estimate=pl.CostEstimate(flops=flops, bytes_accessed=moved, transcendentals=0),
    )(*inputs, *after)


def pack_kernel(
    where_ref, ids_ref, k_ref, v_ref, q_ref, res_ref, out_ref, row_ref, q_out, res_out, ids_vmem, sems
):
    kv = k_ref.shape[1]
    sub = ids_ref.shape[1]
    copies = [
        pltpu.make_async_copy(ids_ref, ids_vmem, sems.at[0]),
        pltpu.make_async_copy(k_ref, out_ref.at[:, :kv], sems.at[1]),
        pltpu.make_async_copy(v_ref, out_ref.at[:, kv:], sems.at[2]),
        pltpu.make_async_copy(q_ref, q_out, sems.at[3]),
        pltpu.make_async_copy(res_ref, res_out, sems.at[4]),
    ]
    for copy in copies:
        copy.start()
    copies[0].wait()
    row = lax.broadcasted_iota(jnp.int32, (TILE, sub), 0)
    two = jnp.where(row == 0, ids_vmem[0:1, :], jnp.where(row == 1, ids_vmem[1:2, :], 0))
    token = lax.broadcasted_iota(jnp.int32, (sub, LANES), 0) + where_ref[1] * sub
    lane = lax.broadcasted_iota(jnp.int32, (sub, LANES), 1)
    place = (token == lane).astype(F32)
    row_ref[...] = jnp.dot(two.astype(F32), place, preferred_element_type=F32).astype(BF16)
    for copy in copies[1:]:
        copy.wait()


def join_kernel(n, *refs):
    spans, rows, (out_ref, row_ref) = refs[:n], refs[n:-2], refs[-2:]
    tok = spans[0].shape[0]
    for d in range(n):
        out_ref[d * tok : (d + 1) * tok, :] = spans[d][...]
    total = rows[0][...].astype(F32)
    for other in rows[1:]:
        total += other[...].astype(F32)
    row_ref[...] = total.astype(BF16)


def attention_kernel(n, where_ref, q_ref, res_ref, near_ref, far_ref, row_ref, hid_ref):
    tok, width = q_ref.shape
    kv = near_ref.shape[1] // 2
    heads = kv // HEAD_WIDTH
    group = width // kv
    ctx = where_ref[0]
    chip, core = ctx // 2, ctx % 2
    own = where_ref[2 + ctx] * tok
    ahead = lax.broadcasted_iota(jnp.int32, (tok, tok), 0) - lax.broadcasted_iota(
        jnp.int32, (tok, tok), 1
    )
    pieces = []
    for side in (core, 1 - core):
        for d in range(n):
            span = 2 * ((chip + d) % n) + side
            pieces.append(jnp.where(ahead >= where_ref[2 + span] * tok - own, 0.0, -1e30))
    bias = jnp.concatenate(pieces, axis=1)
    bias = jnp.concatenate([bias] * group, axis=0)
    for h in range(heads):
        cols = slice(h * HEAD_WIDTH, (h + 1) * HEAD_WIDTH)
        vals = slice(kv + h * HEAD_WIDTH, kv + (h + 1) * HEAD_WIDTH)
        key = jnp.concatenate([near_ref[:, cols], far_ref[:, cols]], axis=0)
        value = jnp.concatenate([near_ref[:, vals], far_ref[:, vals]], axis=0)
        base = h * group * HEAD_WIDTH
        q = jnp.concatenate(
            [q_ref[:, base + g * HEAD_WIDTH : base + (g + 1) * HEAD_WIDTH] for g in range(group)],
            axis=0,
        )
        s = lax.dot_general(q, key, (((1,), (1,)), ((), ())), preferred_element_type=F32)
        s = s * (1.0 / math.sqrt(HEAD_WIDTH)) + bias
        w = jnp.exp(s - jnp.max(s, axis=1, keepdims=True))
        total = jnp.sum(w, axis=1, keepdims=True)
        att = jnp.dot(w.astype(BF16), value, preferred_element_type=F32) / total
        for g in range(group):
            at = slice(base + g * HEAD_WIDTH, base + (g + 1) * HEAD_WIDTH)
            rows = att[g * tok : (g + 1) * tok]
            hid_ref[:tok, at] = (res_ref[:, at].astype(F32) + rows).astype(BF16)
    hid_ref[tok:, :] = jnp.zeros((TILE, width), BF16)
    hid_ref[tok:, :LANES] = row_ref[...]


def pick_kernel(n_exp, slots, tok, n, where_ref, *refs):
    blocks, refs = refs[:n], refs[n:]
    outs, takes, others = refs[:n_exp], refs[n_exp : n_exp + n], refs[n_exp + n :]
    exp = where_ref[1]
    earlier = (
        lax.broadcasted_iota(jnp.int32, (LANES, LANES), 0)
        < lax.broadcasted_iota(jnp.int32, (LANES, LANES), 1)
    ).astype(BF16)
    row = lax.broadcasted_iota(jnp.int32, (TILE, LANES), 0)
    lane = lax.broadcasted_iota(jnp.int32, (TILE, LANES), 1)
    slot = lax.broadcasted_iota(jnp.int32, (slots, LANES), 0).astype(F32)
    target = (exp ^ row).astype(F32)
    chosen = []
    for i in range(n):
        both = blocks[i][tok:, :LANES].astype(F32)
        first, second = both[0:1, :], both[1:2, :]
        sent = jnp.where(((first == target) | (second == target)) & (lane < tok), 1.0, 0.0)
        rank = jnp.dot(sent.astype(BF16), earlier, preferred_element_type=F32)
        chosen.append([])
        for k in range(n_exp):
            one = jnp.where(slot == rank[k : k + 1, :], sent[k : k + 1, :], 0.0)
            take = one[:, :tok].astype(BF16)
            takes[i][k] = take
            chosen[i].append(take)
            if k == 0:
                other = jnp.sum(one * (first + second), axis=1, keepdims=True) - exp.astype(F32)
                others[i][...] = jnp.broadcast_to(other, (slots, LANES))
    for k in range(n_exp):
        rows = [
            jnp.dot(chosen[i][k], blocks[i][:tok, :], preferred_element_type=F32)
            for i in range(n)
        ]
        outs[k][...] = (rows[0] if n == 1 else jnp.concatenate(rows, axis=0)).astype(BF16)


def norm_kernel(n_exp, n, parts, where_ref, gain_ref, router_ref, *refs):
    others, pieces, (out_ref, mix_ref) = refs[:n], refs[n:-2], refs[-2:]
    exp = where_ref[1]
    width = pieces[0].shape[1]
    rows = out_ref.shape[0]

    def load(k):
        held = [pieces[p * n_exp + k][...].astype(F32) for p in range(parts)]
        return held[0] if parts == 1 else jnp.concatenate(held, axis=0)

    square = jnp.zeros((rows, 1), F32)
    for k in range(n_exp):
        x = load(k)
        square += jnp.sum(x * x, axis=1, keepdims=True)
    scale = lax.rsqrt(square * (1.0 / (n_exp * width)) + 1e-05)
    logits = jnp.zeros((rows, router_ref.shape[0]), F32)
    for k in range(n_exp):
        at = pl.ds(pl.multiple_of((exp ^ k) * width, width), width)
        normed = (load(k) * scale * gain_ref[:, at].astype(F32)).astype(BF16)
        out_ref[:, at] = normed
        logits += lax.dot_general(
            normed, router_ref[:, at], (((1,), (1,)), ((), ())), preferred_element_type=F32
        )
    col = lax.broadcasted_iota(jnp.int32, logits.shape, 1)
    other = jnp.concatenate([o[...] for o in others], axis=0)[:, :1]
    own = jnp.sum(jnp.where(col == exp, logits, 0.0), axis=1, keepdims=True)
    rival = jnp.sum(jnp.where(col.astype(F32) == other, logits, 0.0), axis=1, keepdims=True)
    mix = 1.0 / (1.0 + jnp.exp(rival - own))
    mix_ref[...] = jnp.broadcast_to(mix, (rows, LANES))


def up_kernel(n, near_ref, far_ref, g_ref, u_ref, act_ref, x_ref, acc, buf, sems):
    rows = near_ref.shape[0]
    depth = g_ref.shape[1] // n
    slots = buf.shape[0]

    def copy(j):
        part = (g_ref, u_ref)[j // n].at[0, (j % n) * depth : (j % n + 1) * depth, :]
        return pltpu.make_async_copy(part, buf.at[j % slots], sems.at[j % slots])

    for j in range(slots):
        copy(j).start()
    x_ref[:rows, :] = near_ref[...]
    x_ref[rows:, :] = far_ref[...]
    for j in range(2 * n):
        copy(j).wait()
        at = slice((j % n) * depth, (j % n + 1) * depth)
        y = jnp.dot(x_ref[:, at], buf[j % slots], preferred_element_type=F32)
        if j % n == 0:
            acc[j // n] = y
        elif j < 2 * n - 1:
            acc[j // n] += y
        else:
            g = acc[0]
            act_ref[...] = (g * (acc[1] + y) / (1.0 + jnp.exp(-g))).astype(BF16)
        if j + slots < 2 * n:
            copy(j + slots).start()


def down_kernel(ks, where_ref, act_ref, d_ref, near_out, far_out, buf, sems):
    exp = where_ref[1]
    rows = near_out.shape[0]
    width = buf.shape[2]
    copies = []
    for j, k in enumerate(ks):
        at = pl.ds(pl.multiple_of((exp ^ k) * width, width), width)
        copies.append(pltpu.make_async_copy(d_ref.at[0, :, at], buf.at[j], sems.at[j]))
    for copy in copies:
        copy.start()
    for j in range(len(ks)):
        copies[j].wait()
        y = jnp.dot(act_ref[...], buf[j], preferred_element_type=F32).astype(BF16)
        near_out[:, j * width : (j + 1) * width] = y[:rows]
        far_out[:, j * width : (j + 1) * width] = y[rows:]


def scale_kernel(n, near_ref, back_ref, mix_ref, *outs):
    width = outs[0].shape[1]
    mix = mix_ref[:, :1]
    for j in range(n):
        at = slice(j * width, (j + 1) * width)
        both = near_ref[:, at].astype(F32) + back_ref[:, at].astype(F32)
        outs[j][...] = (both * mix).astype(BF16)


def spread_kernel(n_exp, n, *refs):
    takes, parts, outs = refs[:n], refs[n : n + n_exp], refs[n + n_exp :]
    slots = takes[0].shape[1]
    for i in range(n):
        total = None
        for k in range(n_exp):
            rows = parts[k][...].astype(F32)[i * slots : (i + 1) * slots].astype(BF16)
            one = lax.dot_general(
                takes[i][k], rows, (((0,), (0,)), ((), ())), preferred_element_type=F32
            )
            total = one if total is None else total + one
        outs[i][...] = total.astype(outs[i].dtype)


def body(
    queries,
    rotated_keys,
    values,
    residual,
    span_order,
    norm_gain,
    router_weight,
    expert_ids,
    gate_weight,
    up_weight,
    down_weight,
):
    tok, width = queries.shape
    n_ctx, n_exp = lax.axis_size("ctx"), lax.axis_size("exp")
    n_chip = n_ctx // 2
    kv = rotated_keys.shape[1]
    sub = tok // n_exp
    experts = n_exp * gate_weight.shape[0]
    cap = max(2, min(sub, 3 * sub // experts))
    slots = n_exp * cap
    d_model = norm_gain.shape[0]
    where = jnp.concatenate(
        [jnp.stack([lax.axis_index("ctx"), lax.axis_index("exp")]).astype(jnp.int32), span_order]
    )

    def from_chip(x, d):
        pairs = [(2 * ((i // 2 + d) % n_chip) + i % 2, i) for i in range(n_ctx)]
        return lax.ppermute(x, "ctx", pairs) if d else x

    def from_core(x):
        return lax.ppermute(x, "ctx", [(i ^ 1, i) for i in range(n_ctx)])

    def from_peer(x, k):
        return lax.ppermute(x, "exp", [(i ^ k, i) for i in range(n_exp)]) if k else x

    packed, id_row, q_near, res_near = call(
        pack_kernel,
        (
            where,
            *[
                pltpu.with_memory_space_constraint(x, pltpu.HBM)
                for x in (expert_ids.T, rotated_keys, values, queries, residual)
            ],
        ),
        [SMEM] + [ANY] * 5,
        [((tok, 2 * kv), BF16), ((TILE, LANES), BF16)] + [((tok, width), BF16)] * 2,
        4,
        [pltpu.VMEM((2, sub), jnp.int32), pltpu.SemaphoreType.DMA((5,))],
    )
    near = [from_chip(packed, d) for d in range(n_chip)]
    id_rows = [from_peer(id_row, k) for k in range(n_exp)]
    joined, id_all = call(
        functools.partial(join_kernel, n_chip),
        (*near, *id_rows),
        [VMEM] * (n_chip + n_exp),
        [((n_chip * tok, 2 * kv), BF16), ((TILE, LANES), BF16)],
        4,
    )
    score_mib = 4 * width // HEAD_WIDTH * tok * n_ctx * tok // (kv // HEAD_WIDTH) // MIB
    (hidden,) = call(
        functools.partial(attention_kernel, n_chip),
        (where, q_near, res_near, joined, from_core(joined), id_all),
        [SMEM] + [VMEM] * 5,
        [((tok + TILE, width), BF16)],
        8 + 4 * score_mib,
    )
    hidden_units = gate_weight.shape[2]
    gain = norm_gain.reshape(1, d_model)
    router = router_weight.T

    half = n_chip // 2
    forward = list(range(half)) + list(range(n_chip - 1, half - 1, -1))
    groups = [forward[:half], forward[half:]]
    takes, others, pieces = {}, {}, {}

    def pick(ds, blocks, after=()):
        n = len(ds)
        got = call(
            functools.partial(pick_kernel, n_exp, slots, tok, n),
            (where, *blocks),
            [SMEM] + [VMEM] * n,
            [((n * slots, width), BF16)] * n_exp
            + [((n_exp, slots, tok), BF16)] * n
            + [((slots, LANES), F32)] * n,
            10,
            after=after,
        )
        for i, d in enumerate(ds):
            takes[d], others[d] = got[n_exp + i], got[n_exp + n + i]
        pieces[ds[0]] = [from_peer(got[k], k) for k in range(n_exp)]

    messages = [m for m in (groups[0][:1], groups[0][1:], groups[1]) if m]
    pick(messages[0], [hidden])
    arriving = {1: from_chip(hidden, 1)}
    for d in range(2, half):
        arriving[d] = from_chip(arriving[d - 1], 1)
    for d in range(n_chip - 1, half, -1):
        arriving[d] = from_chip(hidden if d == n_chip - 1 else arriving[d + 1], n_chip - 1)
    if half > 1:
        pick(
            messages[1],
            [arriving[d] for d in messages[1]],
            (*pieces[0][1:], arriving[n_chip - 1]),
        )
        arriving[half] = from_chip(arriving[half - 1], 1)
    pick(messages[-1], [arriving[d] for d in messages[-1]])
    picked_all = (others[messages[-1][0]],)

    def take_in(ds, after=()):
        sets = [pieces[d] for d in ds if d in pieces]
        parts = [p for part in sets for p in part]
        rows = len(ds) * slots
        return call(
            functools.partial(norm_kernel, n_exp, len(ds), len(sets)),
            (where, gain, router, *[others[d] for d in ds], *parts),
            [SMEM] + [VMEM] * (2 + len(ds) + len(parts)),
            [((rows, d_model), BF16), ((rows, LANES), F32)],
            12,
            after=after,
        )

    gate_hbm, up_hbm, down_hbm = (
        pltpu.with_memory_space_constraint(w, pltpu.HBM)
        for w in (gate_weight, up_weight, down_weight)
    )

    def run_up(normed, after=()):
        rows = normed.shape[0]
        (act,) = call(
            functools.partial(up_kernel, 4),
            (normed, from_core(normed), gate_hbm, up_hbm),
            [VMEM, VMEM, ANY, ANY],
            [((2 * rows, hidden_units), BF16)],
            26,
            [
                pltpu.VMEM((2 * rows, d_model), BF16),
                pltpu.VMEM((2, 2 * rows, hidden_units), F32),
                pltpu.VMEM((4, d_model // 4, hidden_units), BF16),
                pltpu.SemaphoreType.DMA((4,)),
            ],
            after=after,
        )
        return act

    order = list(range(n_exp))[::-1]
    halves = [order[: n_exp // 2], order[n_exp // 2 :]]

    def run_down(act, ks, after=()):
        return call(
            functools.partial(down_kernel, ks),
            (where, act, down_hbm),
            [SMEM, VMEM, ANY],
            [((act.shape[0] // 2, len(ks) * width), BF16)] * 2,
            12,
            [
                pltpu.VMEM((len(ks), hidden_units, width), BF16),
                pltpu.SemaphoreType.DMA((len(ks),)),
            ],
            after=after,
        )

    def give_back(ks, near_out, far_out, mix, after=()):
        scaled = call(
            functools.partial(scale_kernel, len(ks)),
            (near_out, from_core(far_out), mix),
            [VMEM] * 3,
            [((near_out.shape[0], width), BF16)] * len(ks),
            10,
            after=after,
        )
        return scaled, {k: from_peer(p, k) for k, p in zip(ks, scaled)}

    def lay_out(ds, returned, after=()):
        return call(
            functools.partial(spread_kernel, n_exp, len(ds)),
            (*[takes[d] for d in ds], *[returned[k] for k in range(n_exp)]),
            [VMEM] * (len(ds) + n_exp),
            [((tok, width), F32 if d == 0 else BF16) for d in ds],
            10,
            after=after,
        )

    spread = [None] * n_chip
    normed_a, mix_a = take_in(groups[0], picked_all)
    act_a = run_up(normed_a)
    first_a = run_down(act_a, halves[0])
    normed_b, mix_b = take_in(groups[1], first_a[:1])
    second_a = run_down(act_a, halves[1], (normed_b,))
    scaled, returned_a = give_back(halves[0], *first_a, mix_a)
    more, rest = give_back(halves[1], *second_a, mix_a, scaled[:1])
    returned_a |= rest
    act_b = run_up(normed_b, more[:1])
    first_b = run_down(act_b, halves[0])
    waits = [returned_a[k] for k in range(1, n_exp)]
    second_b = run_down(act_b, halves[1], (first_b[0], *waits))
    scaled, returned_b = give_back(halves[0], *first_b, mix_b)
    more, rest = give_back(halves[1], *second_b, mix_b, scaled[:1])
    returned_b |= rest
    for d, m in zip(groups[0], lay_out(groups[0], returned_a, more[:1])):
        spread[d] = m
    for d, m in zip(groups[1], lay_out(groups[1], returned_b)):
        spread[d] = m
    total = hidden[:tok].astype(F32) + spread[0]
    for d in range(1, n_chip):
        total += from_chip(spread[d], n_chip - d).astype(F32)
    return total.astype(BF16)


def solution(mesh):
    return jax.shard_map(
        body,
        mesh=mesh,
        in_specs=(
            P("ctx", "exp"),
            P("ctx", "exp"),
            P("ctx", "exp"),
            P("ctx", "exp"),
            P(),
            P(),
            P(),
            P(("ctx", "exp"), None),
            P("exp", None, "ctx"),
            P("exp", None, "ctx"),
            P("exp", "ctx", None),
        ),
        out_specs=P("ctx", "exp"),
        check_vma=False,
    )
```

```python
import functools
import math

import jax
import jax.numpy as jnp
from jax import lax
from jax.experimental import pallas as pl
from jax.experimental.pallas import tpu as pltpu
from jax.sharding import PartitionSpec as P

HEAD_WIDTH = 128
TILE = 16
LANES = 128
F32, BF16 = jnp.float32, jnp.bfloat16
MIB = 2**20
VMEM = pl.BlockSpec(memory_space=pltpu.VMEM)
ANY = pl.BlockSpec(memory_space=pl.ANY)
SMEM = pl.BlockSpec(memory_space=pltpu.SMEM)


def call(kernel, inputs, specs, shapes, limit, scratch=(), after=(), kept=()):
    n = len(inputs)

    def ordered(*refs):
        kernel(*refs[:n], *refs[n + len(after) :])

    return pl.pallas_call(
        ordered,
        in_specs=list(specs) + [ANY] * len(after),
        out_specs=[VMEM] * (len(shapes) + len(kept)),
        out_shape=[jax.ShapeDtypeStruct(s, d) for s, d in shapes] + list(kept),
        scratch_shapes=list(scratch),
        compiler_params=pltpu.CompilerParams(vmem_limit_bytes=limit * MIB),
    )(*inputs, *after)


def pack_kernel(
    where_ref, ids_ref, k_ref, v_ref, q_ref, res_ref, out_ref, row_ref, q_out, res_out, ids_vmem, sems
):
    kv = k_ref.shape[1]
    sub = ids_ref.shape[1]
    copies = [
        pltpu.make_async_copy(ids_ref, ids_vmem, sems.at[0]),
        pltpu.make_async_copy(k_ref, out_ref.at[:, :kv], sems.at[1]),
        pltpu.make_async_copy(v_ref, out_ref.at[:, kv:], sems.at[2]),
        pltpu.make_async_copy(q_ref, q_out, sems.at[3]),
        pltpu.make_async_copy(res_ref, res_out, sems.at[4]),
    ]
    for copy in copies:
        copy.start()
    copies[0].wait()
    row = lax.broadcasted_iota(jnp.int32, (TILE, sub), 0)
    two = jnp.where(row == 0, ids_vmem[0:1, :], jnp.where(row == 1, ids_vmem[1:2, :], 0))
    token = lax.broadcasted_iota(jnp.int32, (sub, LANES), 0) + where_ref[1] * sub
    lane = lax.broadcasted_iota(jnp.int32, (sub, LANES), 1)
    place = (token == lane).astype(F32)
    row_ref[...] = jnp.zeros(row_ref.shape, BF16)
    row_ref[:TILE, :LANES] = jnp.dot(
        two.astype(F32), place, preferred_element_type=F32
    ).astype(BF16)
    for copy in copies[1:]:
        copy.wait()


def join_kernel(n, *refs):
    spans, rows, (out_ref, row_ref) = refs[:n], refs[n:-2], refs[-2:]
    tok = spans[0].shape[0]
    for d in range(n):
        out_ref[d * tok : (d + 1) * tok, :] = spans[d][...]
    total = rows[0][:TILE, :LANES].astype(F32)
    for other in rows[1:]:
        total += other[:TILE, :LANES].astype(F32)
    row_ref[...] = total.astype(BF16)


def attention_kernel(n, where_ref, q_ref, res_ref, near_ref, far_ref, row_ref, hid_ref):
    tok, width = q_ref.shape
    kv = near_ref.shape[1] // 2
    heads = kv // HEAD_WIDTH
    group = width // kv
    ctx = where_ref[0]
    chip, core = ctx // 2, ctx % 2
    own = where_ref[2 + ctx] * tok
    ahead = lax.broadcasted_iota(jnp.int32, (tok, tok), 0) - lax.broadcasted_iota(
        jnp.int32, (tok, tok), 1
    )
    pieces = []
    for side in (core, 1 - core):
        for d in range(n):
            span = 2 * ((chip + d) % n) + side
            pieces.append(jnp.where(ahead >= where_ref[2 + span] * tok - own, 0.0, -1e30))
    bias = jnp.concatenate(pieces, axis=1)
    bias = jnp.concatenate([bias] * group, axis=0)
    for h in range(heads):
        cols = slice(h * HEAD_WIDTH, (h + 1) * HEAD_WIDTH)
        vals = slice(kv + h * HEAD_WIDTH, kv + (h + 1) * HEAD_WIDTH)
        key = jnp.concatenate([near_ref[:, cols], far_ref[:, cols]], axis=0)
        value = jnp.concatenate([near_ref[:, vals], far_ref[:, vals]], axis=0)
        base = h * group * HEAD_WIDTH
        q = jnp.concatenate(
            [q_ref[:, base + g * HEAD_WIDTH : base + (g + 1) * HEAD_WIDTH] for g in range(group)],
            axis=0,
        )
        s = lax.dot_general(q, key, (((1,), (1,)), ((), ())), preferred_element_type=F32)
        s = s * (1.0 / math.sqrt(HEAD_WIDTH)) + bias
        w = jnp.exp(s - jnp.max(s, axis=1, keepdims=True))
        total = jnp.sum(w, axis=1, keepdims=True)
        att = jnp.dot(w.astype(BF16), value, preferred_element_type=F32) / total
        for g in range(group):
            at = slice(base + g * HEAD_WIDTH, base + (g + 1) * HEAD_WIDTH)
            rows = att[g * tok : (g + 1) * tok]
            hid_ref[:tok, at] = (res_ref[:, at].astype(F32) + rows).astype(BF16)
    hid_ref[tok:, :] = jnp.zeros((TILE, width), BF16)
    hid_ref[tok:, :LANES] = row_ref[...]


def pick_kernel(n_exp, slots, tok, n, where_ref, *refs):
    blocks, refs = refs[:n], refs[n:]
    outs, takes, others = refs[:n_exp], refs[n_exp : n_exp + n], refs[n_exp + n :]
    exp = where_ref[1]
    earlier = (
        lax.broadcasted_iota(jnp.int32, (LANES, LANES), 0)
        < lax.broadcasted_iota(jnp.int32, (LANES, LANES), 1)
    ).astype(BF16)
    row = lax.broadcasted_iota(jnp.int32, (TILE, LANES), 0)
    lane = lax.broadcasted_iota(jnp.int32, (TILE, LANES), 1)
    slot = lax.broadcasted_iota(jnp.int32, (slots, LANES), 0).astype(F32)
    target = (exp ^ row).astype(F32)
    chosen = []
    for i in range(n):
        both = blocks[i][tok:, :LANES].astype(F32)
        first, second = both[0:1, :], both[1:2, :]
        sent = jnp.where(((first == target) | (second == target)) & (lane < tok), 1.0, 0.0)
        rank = jnp.dot(sent.astype(BF16), earlier, preferred_element_type=F32)
        chosen.append([])
        for k in range(n_exp):
            one = jnp.where(slot == rank[k : k + 1, :], sent[k : k + 1, :], 0.0)
            take = one[:, :tok].astype(BF16)
            takes[i][k] = take
            chosen[i].append(take)
            if k == 0:
                other = jnp.sum(one * (first + second), axis=1, keepdims=True) - exp.astype(F32)
                others[i][...] = jnp.broadcast_to(other, (slots, LANES))
    for k in range(n_exp):
        rows = [
            jnp.dot(chosen[i][k], blocks[i][:tok, :], preferred_element_type=F32)
            for i in range(n)
        ]
        outs[k][...] = (rows[0] if n == 1 else jnp.concatenate(rows, axis=0)).astype(BF16)


def norm_kernel(n_exp, n, parts, where_ref, gain_ref, router_ref, *refs):
    others, pieces, (out_ref, mix_ref) = refs[:n], refs[n:-2], refs[-2:]
    exp = where_ref[1]
    width = pieces[0].shape[1]
    rows = out_ref.shape[0]

    def load(k):
        held = [pieces[p * n_exp + k][...].astype(F32) for p in range(parts)]
        return held[0] if parts == 1 else jnp.concatenate(held, axis=0)

    square = jnp.zeros((rows, 1), F32)
    for k in range(n_exp):
        x = load(k)
        square += jnp.sum(x * x, axis=1, keepdims=True)
    scale = lax.rsqrt(square * (1.0 / (n_exp * width)) + 1e-05)
    logits = jnp.zeros((rows, router_ref.shape[0]), F32)
    for k in range(n_exp):
        at = pl.ds(pl.multiple_of((exp ^ k) * width, width), width)
        normed = (load(k) * scale * gain_ref[:, at].astype(F32)).astype(BF16)
        out_ref[:, at] = normed
        logits += lax.dot_general(
            normed, router_ref[:, at], (((1,), (1,)), ((), ())), preferred_element_type=F32
        )
    col = lax.broadcasted_iota(jnp.int32, logits.shape, 1)
    other = jnp.concatenate([o[...] for o in others], axis=0)[:, :1]
    own = jnp.sum(jnp.where(col == exp, logits, 0.0), axis=1, keepdims=True)
    rival = jnp.sum(jnp.where(col.astype(F32) == other, logits, 0.0), axis=1, keepdims=True)
    mix = 1.0 / (1.0 + jnp.exp(rival - own))
    mix_ref[...] = jnp.broadcast_to(mix, (rows, LANES))


def up_kernel(n, fetch, near_ref, far_ref, g_ref, u_ref, act_ref, *refs):
    kept, (x_ref, acc, sems) = refs[:-3], refs[-3:]
    held = kept if fetch else (g_ref, u_ref)
    rows = near_ref.shape[0]
    depth = held[0].shape[0] // n
    at = [slice(j * depth, (j + 1) * depth) for j in range(n)]
    copies = []
    if fetch:
        copies = [
            pltpu.make_async_copy(w.at[0, part], v.at[part], sems.at[i * n + j])
            for i, (w, v) in enumerate(((g_ref, kept[0]), (u_ref, kept[1])))
            for j, part in enumerate(at)
        ]
    for copy in copies:
        copy.start()
    x_ref[:rows, :] = near_ref[...]
    x_ref[rows:, :] = far_ref[...]
    for j in range(2 * n):
        if fetch:
            copies[j].wait()
        part = at[j % n]
        y = jnp.dot(x_ref[:, part], held[j // n][part, :], preferred_element_type=F32)
        if j % n == 0:
            acc[j // n] = y
        elif j < 2 * n - 1:
            acc[j // n] += y
        else:
            g = acc[0]
            act_ref[...] = (g * (acc[1] + y) / (1.0 + jnp.exp(-g))).astype(BF16)


def down_kernel(ks, fetch, where_ref, act_ref, d_ref, near_out, far_out, *refs):
    kept, sems = refs[:-1], refs[-1]
    held = kept[0] if fetch else d_ref
    exp = where_ref[1]
    rows = near_out.shape[0]
    width = held.shape[2]
    copies = []
    if fetch:
        for j, k in enumerate(ks):
            at = pl.ds(pl.multiple_of((exp ^ k) * width, width), width)
            copies.append(pltpu.make_async_copy(d_ref.at[0, :, at], held.at[j], sems.at[j]))
    for copy in copies:
        copy.start()
    for j in range(len(ks)):
        if fetch:
            copies[j].wait()
        y = jnp.dot(act_ref[...], held[j], preferred_element_type=F32).astype(BF16)
        near_out[:, j * width : (j + 1) * width] = y[:rows]
        far_out[:, j * width : (j + 1) * width] = y[rows:]


def scale_kernel(n, near_ref, back_ref, mix_ref, *outs):
    width = outs[0].shape[1]
    mix = mix_ref[:, :1]
    for j in range(n):
        at = slice(j * width, (j + 1) * width)
        both = near_ref[:, at].astype(F32) + back_ref[:, at].astype(F32)
        outs[j][...] = (both * mix).astype(BF16)


def spread_kernel(n_exp, n, *refs):
    takes, parts, outs = refs[:n], refs[n : n + n_exp], refs[n + n_exp :]
    slots = takes[0].shape[1]
    for i in range(n):
        total = None
        for k in range(n_exp):
            rows = parts[k][...].astype(F32)[i * slots : (i + 1) * slots].astype(BF16)
            one = lax.dot_general(
                takes[i][k], rows, (((0,), (0,)), ((), ())), preferred_element_type=F32
            )
            total = one if total is None else total + one
        outs[i][...] = total.astype(outs[i].dtype)


def body(
    queries,
    rotated_keys,
    values,
    residual,
    span_order,
    norm_gain,
    router_weight,
    expert_ids,
    gate_weight,
    up_weight,
    down_weight,
):
    tok, width = queries.shape
    n_ctx, n_exp = lax.axis_size("ctx"), lax.axis_size("exp")
    n_chip = n_ctx // 2
    kv = rotated_keys.shape[1]
    sub = tok // n_exp
    experts = n_exp * gate_weight.shape[0]
    cap = max(2, min(sub, 3 * sub // experts))
    slots = n_exp * cap
    d_model = norm_gain.shape[0]
    where = jnp.concatenate(
        [jnp.stack([lax.axis_index("ctx"), lax.axis_index("exp")]).astype(jnp.int32), span_order]
    )

    def from_chip(x, d):
        pairs = [(2 * ((i // 2 + d) % n_chip) + i % 2, i) for i in range(n_ctx)]
        return lax.ppermute(x, "ctx", pairs) if d else x

    def from_core(x):
        return lax.ppermute(x, "ctx", [(i ^ 1, i) for i in range(n_ctx)])

    def from_peer(x, k):
        return lax.ppermute(x, "exp", [(i ^ k, i) for i in range(n_exp)]) if k else x

    packed, id_row, q_near, res_near = call(
        pack_kernel,
        (
            where,
            *[
                pltpu.with_memory_space_constraint(x, pltpu.HBM)
                for x in (expert_ids.T, rotated_keys, values, queries, residual)
            ],
        ),
        [SMEM] + [ANY] * 5,
        [((tok, 2 * kv), BF16)] * 2 + [((tok, width), BF16)] * 2,
        4,
        [pltpu.VMEM((2, sub), jnp.int32), pltpu.SemaphoreType.DMA((5,))],
    )
    near = [from_chip(packed, d) for d in range(n_chip)]
    id_rows = [from_peer(id_row, k) for k in range(n_exp)]
    joined, id_all = call(
        functools.partial(join_kernel, n_chip),
        (*near, *id_rows),
        [VMEM] * (n_chip + n_exp),
        [((n_chip * tok, 2 * kv), BF16), ((TILE, LANES), BF16)],
        4,
    )
    score_mib = 4 * width // HEAD_WIDTH * tok * n_ctx * tok // (kv // HEAD_WIDTH) // MIB
    (hidden,) = call(
        functools.partial(attention_kernel, n_chip),
        (where, q_near, res_near, joined, from_core(joined), id_all),
        [SMEM] + [VMEM] * 5,
        [((tok + TILE, width), BF16)],
        8 + 4 * score_mib,
    )
    hidden_units = gate_weight.shape[2]
    gain = norm_gain.reshape(1, d_model)
    router = router_weight.T

    half = n_chip // 2
    forward = list(range(half)) + list(range(n_chip - 1, half - 1, -1))
    groups = [forward[:half], forward[half:]]
    takes, others, pieces = {}, {}, {}

    def pick(ds, blocks, after=()):
        n = len(ds)
        got = call(
            functools.partial(pick_kernel, n_exp, slots, tok, n),
            (where, *blocks),
            [SMEM] + [VMEM] * n,
            [((n * slots, width), BF16)] * n_exp
            + [((n_exp, slots, tok), BF16)] * n
            + [((slots, LANES), F32)] * n,
            10,
            after=after,
        )
        for i, d in enumerate(ds):
            takes[d], others[d] = got[n_exp + i], got[n_exp + n + i]
        pieces[ds[0]] = [from_peer(got[k], k) for k in range(n_exp)]

    messages = [m for m in (groups[0][:1], groups[0][1:], groups[1]) if m]
    pick(messages[0], [hidden])
    arriving = {1: from_chip(hidden, 1)}
    for d in range(2, half):
        arriving[d] = from_chip(arriving[d - 1], 1)
    for d in range(n_chip - 1, half, -1):
        arriving[d] = from_chip(hidden if d == n_chip - 1 else arriving[d + 1], n_chip - 1)
    if half > 1:
        pick(
            messages[1],
            [arriving[d] for d in messages[1]],
            (*pieces[0][1:], arriving[n_chip - 1]),
        )
        arriving[half] = from_chip(arriving[half - 1], 1)
    pick(messages[-1], [arriving[d] for d in messages[-1]])
    picked_all = (others[messages[-1][0]],)

    def take_in(ds, after=()):
        sets = [pieces[d] for d in ds if d in pieces]
        parts = [p for part in sets for p in part]
        rows = len(ds) * slots
        return call(
            functools.partial(norm_kernel, n_exp, len(ds), len(sets)),
            (where, gain, router, *[others[d] for d in ds], *parts),
            [SMEM] + [VMEM] * (2 + len(ds) + len(parts)),
            [((rows, d_model), BF16), ((rows, LANES), F32)],
            8,
            after=after,
        )

    gate_hbm, up_hbm, down_hbm = (
        pltpu.with_memory_space_constraint(w, pltpu.HBM)
        for w in (gate_weight, up_weight, down_weight)
    )

    n_part = 4
    weights = {}

    def run_up(normed, after=()):
        rows = normed.shape[0]
        fetch = "up" not in weights
        spec = ANY if fetch else VMEM
        act, *kept = call(
            functools.partial(up_kernel, n_part, fetch),
            (normed, from_core(normed), *(weights["up"] if not fetch else (gate_hbm, up_hbm))),
            [VMEM, VMEM, spec, spec],
            [((2 * rows, hidden_units), BF16)],
            10,
            [
                pltpu.VMEM((2 * rows, d_model), BF16),
                pltpu.VMEM((2, 2 * rows, hidden_units), F32),
                pltpu.SemaphoreType.DMA((2 * n_part,)),
            ],
            after=after,
            kept=[pltpu.VMEM((d_model, hidden_units), BF16)] * (2 * fetch),
        )
        if fetch:
            weights["up"] = kept
        return act

    order = list(range(n_exp))[::-1]
    halves = [order[: n_exp // 2], order[n_exp // 2 :]]

    def run_down(act, ks, after=()):
        fetch = ks[0] not in weights
        near_out, far_out, *kept = call(
            functools.partial(down_kernel, ks, fetch),
            (where, act, down_hbm if fetch else weights[ks[0]]),
            [SMEM, VMEM, ANY if fetch else VMEM],
            [((act.shape[0] // 2, len(ks) * width), BF16)] * 2,
            6,
            [pltpu.SemaphoreType.DMA((len(ks),))],
            after=after,
            kept=[pltpu.VMEM((len(ks), hidden_units, width), BF16)] * fetch,
        )
        if fetch:
            weights[ks[0]] = kept[0]
        return near_out, far_out

    def give_back(ks, near_out, far_out, mix, after=()):
        scaled = call(
            functools.partial(scale_kernel, len(ks)),
            (near_out, from_core(far_out), mix),
            [VMEM] * 3,
            [((near_out.shape[0], width), BF16)] * len(ks),
            10,
            after=after,
        )
        return scaled, {k: from_peer(p, k) for k, p in zip(ks, scaled)}

    def lay_out(ds, returned, after=()):
        return call(
            functools.partial(spread_kernel, n_exp, len(ds)),
            (*[takes[d] for d in ds], *[returned[k] for k in range(n_exp)]),
            [VMEM] * (len(ds) + n_exp),
            [((tok, width), F32 if d == 0 else BF16) for d in ds],
            10,
            after=after,
        )

    spread = [None] * n_chip
    normed_a, mix_a = take_in(groups[0], picked_all)
    act_a = run_up(normed_a)
    first_a = run_down(act_a, halves[0])
    normed_b, mix_b = take_in(groups[1], first_a[:1])
    second_a = run_down(act_a, halves[1], (normed_b,))
    scaled, returned_a = give_back(halves[0], *first_a, mix_a)
    more, rest = give_back(halves[1], *second_a, mix_a, scaled[:1])
    returned_a |= rest
    act_b = run_up(normed_b, more[:1])
    first_b = run_down(act_b, halves[0])
    waits = [returned_a[n_exp - 1]]
    second_b = run_down(act_b, halves[1], (first_b[0], *waits))
    scaled, returned_b = give_back(halves[0], *first_b, mix_b)
    more, rest = give_back(halves[1], *second_b, mix_b, scaled[:1])
    returned_b |= rest
    for d, m in zip(groups[0], lay_out(groups[0], returned_a, more[:1])):
        spread[d] = m
    for d, m in zip(groups[1], lay_out(groups[1], returned_b)):
        spread[d] = m
    total = hidden[:tok].astype(F32) + spread[0]
    for d in range(1, n_chip):
        total += from_chip(spread[d], n_chip - d).astype(F32)
    return total.astype(BF16)


def solution(mesh):
    return jax.shard_map(
        body,
        mesh=mesh,
        in_specs=(
            P("ctx", "exp"),
            P("ctx", "exp"),
            P("ctx", "exp"),
            P("ctx", "exp"),
            P(),
            P(),
            P(),
            P(("ctx", "exp"), None),
            P("exp", None, "ctx"),
            P("exp", None, "ctx"),
            P("exp", "ctx", None),
        ),
        out_specs=P("ctx", "exp"),
        check_vma=False,
    )
```

```python
import functools
import math

import jax
import jax.numpy as jnp
from jax import lax
from jax.experimental import pallas as pl
from jax.experimental.pallas import tpu as pltpu
from jax.sharding import PartitionSpec as P

HEAD_WIDTH = 128
TILE = 16
LANES = 128
F32, BF16 = jnp.float32, jnp.bfloat16
MIB = 2**20
VMEM = pl.BlockSpec(memory_space=pltpu.VMEM)
ANY = pl.BlockSpec(memory_space=pl.ANY)
SMEM = pl.BlockSpec(memory_space=pltpu.SMEM)


def call(kernel, inputs, specs, shapes, limit, scratch=(), after=(), kept=()):
    n = len(inputs)

    def ordered(*refs):
        kernel(*refs[:n], *refs[n + len(after) :])

    return pl.pallas_call(
        ordered,
        in_specs=list(specs) + [ANY] * len(after),
        out_specs=[VMEM] * (len(shapes) + len(kept)),
        out_shape=[jax.ShapeDtypeStruct(s, d) for s, d in shapes] + list(kept),
        scratch_shapes=list(scratch),
        compiler_params=pltpu.CompilerParams(vmem_limit_bytes=limit * MIB),
    )(*inputs, *after)


def pack_kernel(
    where_ref, ids_ref, k_ref, v_ref, q_ref, res_ref, out_ref, row_ref, q_out, res_out, ids_vmem, sems
):
    kv = k_ref.shape[1]
    sub = ids_ref.shape[1]
    copies = [
        pltpu.make_async_copy(ids_ref, ids_vmem, sems.at[0]),
        pltpu.make_async_copy(k_ref, out_ref.at[:, :kv], sems.at[1]),
        pltpu.make_async_copy(v_ref, out_ref.at[:, kv:], sems.at[2]),
        pltpu.make_async_copy(q_ref, q_out, sems.at[3]),
        pltpu.make_async_copy(res_ref, res_out, sems.at[4]),
    ]
    for copy in copies:
        copy.start()
    copies[0].wait()
    row = lax.broadcasted_iota(jnp.int32, (TILE, sub), 0)
    two = jnp.where(row == 0, ids_vmem[0:1, :], jnp.where(row == 1, ids_vmem[1:2, :], 0))
    token = lax.broadcasted_iota(jnp.int32, (sub, LANES), 0) + where_ref[1] * sub
    lane = lax.broadcasted_iota(jnp.int32, (sub, LANES), 1)
    place = (token == lane).astype(F32)
    row_ref[...] = jnp.zeros(row_ref.shape, BF16)
    row_ref[:TILE, :LANES] = jnp.dot(
        two.astype(F32), place, preferred_element_type=F32
    ).astype(BF16)
    for copy in copies[1:]:
        copy.wait()


def join_kernel(n, *refs):
    spans, rows, (out_ref, row_ref) = refs[:n], refs[n:-2], refs[-2:]
    tok = spans[0].shape[0]
    for d in range(n):
        out_ref[d * tok : (d + 1) * tok, :] = spans[d][...]
    total = rows[0][:TILE, :LANES].astype(F32)
    for other in rows[1:]:
        total += other[:TILE, :LANES].astype(F32)
    row_ref[...] = total.astype(BF16)


def attention_kernel(n, where_ref, q_ref, res_ref, near_ref, far_ref, row_ref, hid_ref):
    tok, width = q_ref.shape
    kv = near_ref.shape[1] // 2
    heads = kv // HEAD_WIDTH
    group = width // kv
    ctx = where_ref[0]
    chip, core = ctx // 2, ctx % 2
    own = where_ref[2 + ctx] * tok
    ahead = lax.broadcasted_iota(jnp.int32, (tok, tok), 0) - lax.broadcasted_iota(
        jnp.int32, (tok, tok), 1
    )
    pieces = []
    for side in (core, 1 - core):
        for d in range(n):
            span = 2 * ((chip + d) % n) + side
            pieces.append(jnp.where(ahead >= where_ref[2 + span] * tok - own, 0.0, -1e30))
    bias = jnp.concatenate(pieces, axis=1)
    bias = jnp.concatenate([bias] * group, axis=0)
    for h in range(heads):
        cols = slice(h * HEAD_WIDTH, (h + 1) * HEAD_WIDTH)
        vals = slice(kv + h * HEAD_WIDTH, kv + (h + 1) * HEAD_WIDTH)
        key = jnp.concatenate([near_ref[:, cols], far_ref[:, cols]], axis=0)
        value = jnp.concatenate([near_ref[:, vals], far_ref[:, vals]], axis=0)
        base = h * group * HEAD_WIDTH
        q = jnp.concatenate(
            [q_ref[:, base + g * HEAD_WIDTH : base + (g + 1) * HEAD_WIDTH] for g in range(group)],
            axis=0,
        )
        s = lax.dot_general(q, key, (((1,), (1,)), ((), ())), preferred_element_type=F32)
        s = s * (1.0 / math.sqrt(HEAD_WIDTH)) + bias
        w = jnp.exp(s - jnp.max(s, axis=1, keepdims=True))
        total = jnp.sum(w, axis=1, keepdims=True)
        att = jnp.dot(w.astype(BF16), value, preferred_element_type=F32) / total
        for g in range(group):
            at = slice(base + g * HEAD_WIDTH, base + (g + 1) * HEAD_WIDTH)
            rows = att[g * tok : (g + 1) * tok]
            hid_ref[:tok, at] = (res_ref[:, at].astype(F32) + rows).astype(BF16)
    hid_ref[tok:, :] = jnp.zeros((TILE, width), BF16)
    hid_ref[tok:, :LANES] = row_ref[...]


def pick_kernel(n_exp, slots, tok, n, where_ref, *refs):
    blocks, refs = refs[:n], refs[n:]
    outs, takes, others = refs[:n_exp], refs[n_exp : n_exp + n], refs[n_exp + n :]
    exp = where_ref[1]
    earlier = (
        lax.broadcasted_iota(jnp.int32, (LANES, LANES), 0)
        < lax.broadcasted_iota(jnp.int32, (LANES, LANES), 1)
    ).astype(BF16)
    row = lax.broadcasted_iota(jnp.int32, (TILE, LANES), 0)
    lane = lax.broadcasted_iota(jnp.int32, (TILE, LANES), 1)
    slot = lax.broadcasted_iota(jnp.int32, (slots, LANES), 0).astype(F32)
    target = (exp ^ row).astype(F32)
    chosen = []
    for i in range(n):
        both = blocks[i][tok:, :LANES].astype(F32)
        first, second = both[0:1, :], both[1:2, :]
        sent = jnp.where(((first == target) | (second == target)) & (lane < tok), 1.0, 0.0)
        rank = jnp.dot(sent.astype(BF16), earlier, preferred_element_type=F32)
        chosen.append([])
        for k in range(n_exp):
            one = jnp.where(slot == rank[k : k + 1, :], sent[k : k + 1, :], 0.0)
            take = one[:, :tok].astype(BF16)
            takes[i][k] = take
            chosen[i].append(take)
            if k == 0:
                other = jnp.sum(one * (first + second), axis=1, keepdims=True) - exp.astype(F32)
                others[i][...] = jnp.broadcast_to(other, (slots, LANES))
    for k in range(n_exp):
        rows = [
            jnp.dot(chosen[i][k], blocks[i][:tok, :], preferred_element_type=F32)
            for i in range(n)
        ]
        outs[k][...] = (rows[0] if n == 1 else jnp.concatenate(rows, axis=0)).astype(BF16)


def norm_kernel(n_exp, n, parts, where_ref, gain_ref, router_ref, *refs):
    others, pieces, (out_ref, mix_ref) = refs[:n], refs[n:-2], refs[-2:]
    exp = where_ref[1]
    width = pieces[0].shape[1]
    rows = out_ref.shape[0]

    def load(k):
        held = [pieces[p * n_exp + k][...].astype(F32) for p in range(parts)]
        return held[0] if parts == 1 else jnp.concatenate(held, axis=0)

    square = jnp.zeros((rows, 1), F32)
    for k in range(n_exp):
        x = load(k)
        square += jnp.sum(x * x, axis=1, keepdims=True)
    scale = lax.rsqrt(square * (1.0 / (n_exp * width)) + 1e-05)
    logits = jnp.zeros((rows, router_ref.shape[0]), F32)
    for k in range(n_exp):
        at = pl.ds(pl.multiple_of((exp ^ k) * width, width), width)
        normed = (load(k) * scale * gain_ref[:, at].astype(F32)).astype(BF16)
        out_ref[:, at] = normed
        logits += lax.dot_general(
            normed, router_ref[:, at], (((1,), (1,)), ((), ())), preferred_element_type=F32
        )
    col = lax.broadcasted_iota(jnp.int32, logits.shape, 1)
    other = jnp.concatenate([o[...] for o in others], axis=0)[:, :1]
    own = jnp.sum(jnp.where(col == exp, logits, 0.0), axis=1, keepdims=True)
    rival = jnp.sum(jnp.where(col.astype(F32) == other, logits, 0.0), axis=1, keepdims=True)
    mix = 1.0 / (1.0 + jnp.exp(rival - own))
    mix_ref[...] = jnp.broadcast_to(mix, (rows, LANES))


def up_kernel(n, fetch, near_ref, far_ref, g_ref, u_ref, act_ref, *refs):
    kept, (x_ref, acc, sems) = refs[:-3], refs[-3:]
    held = kept if fetch else (g_ref, u_ref)
    rows = near_ref.shape[0]
    depth = held[0].shape[0] // n
    at = [slice(j * depth, (j + 1) * depth) for j in range(n)]
    copies = []
    if fetch:
        copies = [
            pltpu.make_async_copy(w.at[0, part], v.at[part], sems.at[i * n + j])
            for i, (w, v) in enumerate(((g_ref, kept[0]), (u_ref, kept[1])))
            for j, part in enumerate(at)
        ]
    for copy in copies:
        copy.start()
    x_ref[:rows, :] = near_ref[...]
    x_ref[rows:, :] = far_ref[...]
    for j in range(2 * n):
        if fetch:
            copies[j].wait()
        part = at[j % n]
        y = jnp.dot(x_ref[:, part], held[j // n][part, :], preferred_element_type=F32)
        if j % n == 0:
            acc[j // n] = y
        elif j < 2 * n - 1:
            acc[j // n] += y
        else:
            g = acc[0]
            act_ref[...] = (g * (acc[1] + y) / (1.0 + jnp.exp(-g))).astype(BF16)


def down_kernel(ks, fetch, where_ref, act_ref, d_ref, near_out, far_out, *refs):
    kept, sems = refs[:-1], refs[-1]
    held = kept[0] if fetch else d_ref
    exp = where_ref[1]
    rows = near_out.shape[0]
    width = held.shape[2]
    copies = []
    if fetch:
        for j, k in enumerate(ks):
            at = pl.ds(pl.multiple_of((exp ^ k) * width, width), width)
            copies.append(pltpu.make_async_copy(d_ref.at[0, :, at], held.at[j], sems.at[j]))
    for copy in copies:
        copy.start()
    for j in range(len(ks)):
        if fetch:
            copies[j].wait()
        y = jnp.dot(act_ref[...], held[j], preferred_element_type=F32).astype(BF16)
        near_out[:, j * width : (j + 1) * width] = y[:rows]
        far_out[:, j * width : (j + 1) * width] = y[rows:]


def scale_kernel(n, near_ref, back_ref, mix_ref, *outs):
    width = outs[0].shape[1]
    mix = mix_ref[:, :1]
    for j in range(n):
        at = slice(j * width, (j + 1) * width)
        both = near_ref[:, at].astype(F32) + back_ref[:, at].astype(F32)
        outs[j][...] = (both * mix).astype(BF16)


def spread_kernel(n_exp, n, *refs):
    takes, parts, outs = refs[:n], refs[n : n + n_exp], refs[n + n_exp :]
    slots = takes[0].shape[1]
    for i in range(n):
        total = None
        for k in range(n_exp):
            rows = parts[k][...].astype(F32)[i * slots : (i + 1) * slots].astype(BF16)
            one = lax.dot_general(
                takes[i][k], rows, (((0,), (0,)), ((), ())), preferred_element_type=F32
            )
            total = one if total is None else total + one
        outs[i][...] = total.astype(outs[i].dtype)


def body(
    queries,
    rotated_keys,
    values,
    residual,
    span_order,
    norm_gain,
    router_weight,
    expert_ids,
    gate_weight,
    up_weight,
    down_weight,
):
    tok, width = queries.shape
    n_ctx, n_exp = lax.axis_size("ctx"), lax.axis_size("exp")
    n_chip = n_ctx // 2
    kv = rotated_keys.shape[1]
    sub = tok // n_exp
    experts = n_exp * gate_weight.shape[0]
    cap = max(2, min(sub, 3 * sub // experts))
    slots = n_exp * cap
    d_model = norm_gain.shape[0]
    where = jnp.concatenate(
        [jnp.stack([lax.axis_index("ctx"), lax.axis_index("exp")]).astype(jnp.int32), span_order]
    )

    def from_chip(x, d):
        pairs = [(2 * ((i // 2 + d) % n_chip) + i % 2, i) for i in range(n_ctx)]
        return lax.ppermute(x, "ctx", pairs) if d else x

    def from_core(x):
        return lax.ppermute(x, "ctx", [(i ^ 1, i) for i in range(n_ctx)])

    def from_peer(x, k):
        return lax.ppermute(x, "exp", [(i ^ k, i) for i in range(n_exp)]) if k else x

    packed, id_row, q_near, res_near = call(
        pack_kernel,
        (
            where,
            *[
                pltpu.with_memory_space_constraint(x, pltpu.HBM)
                for x in (expert_ids.T, rotated_keys, values, queries, residual)
            ],
        ),
        [SMEM] + [ANY] * 5,
        [((tok, 2 * kv), BF16)] * 2 + [((tok, width), BF16)] * 2,
        4,
        [pltpu.VMEM((2, sub), jnp.int32), pltpu.SemaphoreType.DMA((5,))],
    )
    near = [from_chip(packed, d) for d in range(n_chip)]
    id_rows = [from_peer(id_row, k) for k in range(n_exp)]
    joined, id_all = call(
        functools.partial(join_kernel, n_chip),
        (*near, *id_rows),
        [VMEM] * (n_chip + n_exp),
        [((n_chip * tok, 2 * kv), BF16), ((TILE, LANES), BF16)],
        4,
    )
    score_mib = 4 * width // HEAD_WIDTH * tok * n_ctx * tok // (kv // HEAD_WIDTH) // MIB
    (hidden,) = call(
        functools.partial(attention_kernel, n_chip),
        (where, q_near, res_near, joined, from_core(joined), id_all),
        [SMEM] + [VMEM] * 5,
        [((tok + TILE, width), BF16)],
        8 + 4 * score_mib,
    )
    hidden_units = gate_weight.shape[2]
    gain = norm_gain.reshape(1, d_model)
    router = router_weight.T

    half = n_chip // 2
    forward = list(range(half)) + list(range(n_chip - 1, half - 1, -1))
    groups = [forward[:half], forward[half:]]
    takes, others, pieces = {}, {}, {}

    def pick(ds, blocks, after=()):
        n = len(ds)
        got = call(
            functools.partial(pick_kernel, n_exp, slots, tok, n),
            (where, *blocks),
            [SMEM] + [VMEM] * n,
            [((n * slots, width), BF16)] * n_exp
            + [((n_exp, slots, tok), BF16)] * n
            + [((slots, LANES), F32)] * n,
            10,
            after=after,
        )
        for i, d in enumerate(ds):
            takes[d], others[d] = got[n_exp + i], got[n_exp + n + i]
        pieces[ds[0]] = [from_peer(got[k], k) for k in range(n_exp)]

    messages = [m for m in (groups[0][:1], groups[0][1:], groups[1]) if m]
    pick(messages[0], [hidden])
    arriving = {1: from_chip(hidden, 1)}
    for d in range(2, half):
        arriving[d] = from_chip(arriving[d - 1], 1)
    for d in range(n_chip - 1, half, -1):
        arriving[d] = from_chip(hidden if d == n_chip - 1 else arriving[d + 1], n_chip - 1)
    if half > 1:
        pick(
            messages[1],
            [arriving[d] for d in messages[1]],
            (*pieces[0][1:],),
        )
        arriving[half] = from_chip(arriving[half - 1], 1)
    pick(messages[-1], [arriving[d] for d in messages[-1]])
    picked_all = (others[messages[-1][0]],)

    def take_in(ds, after=()):
        sets = [pieces[d] for d in ds if d in pieces]
        parts = [p for part in sets for p in part]
        rows = len(ds) * slots
        return call(
            functools.partial(norm_kernel, n_exp, len(ds), len(sets)),
            (where, gain, router, *[others[d] for d in ds], *parts),
            [SMEM] + [VMEM] * (2 + len(ds) + len(parts)),
            [((rows, d_model), BF16), ((rows, LANES), F32)],
            8,
            after=after,
        )

    gate_hbm, up_hbm, down_hbm = (
        pltpu.with_memory_space_constraint(w, pltpu.HBM)
        for w in (gate_weight, up_weight, down_weight)
    )

    n_part = 4
    weights = {}

    def run_up(normed, after=()):
        rows = normed.shape[0]
        fetch = "up" not in weights
        spec = ANY if fetch else VMEM
        act, *kept = call(
            functools.partial(up_kernel, n_part, fetch),
            (normed, from_core(normed), *(weights["up"] if not fetch else (gate_hbm, up_hbm))),
            [VMEM, VMEM, spec, spec],
            [((2 * rows, hidden_units), BF16)],
            10,
            [
                pltpu.VMEM((2 * rows, d_model), BF16),
                pltpu.VMEM((2, 2 * rows, hidden_units), F32),
                pltpu.SemaphoreType.DMA((2 * n_part,)),
            ],
            after=after,
            kept=[pltpu.VMEM((d_model, hidden_units), BF16)] * (2 * fetch),
        )
        if fetch:
            weights["up"] = kept
        return act

    order = list(range(n_exp))[::-1]
    halves = [order[: n_exp // 2], order[n_exp // 2 :]]

    def run_down(act, ks, after=()):
        fetch = ks[0] not in weights
        near_out, far_out, *kept = call(
            functools.partial(down_kernel, ks, fetch),
            (where, act, down_hbm if fetch else weights[ks[0]]),
            [SMEM, VMEM, ANY if fetch else VMEM],
            [((act.shape[0] // 2, len(ks) * width), BF16)] * 2,
            6,
            [pltpu.SemaphoreType.DMA((len(ks),))],
            after=after,
            kept=[pltpu.VMEM((len(ks), hidden_units, width), BF16)] * fetch,
        )
        if fetch:
            weights[ks[0]] = kept[0]
        return near_out, far_out

    def give_back(ks, near_out, far_out, mix, after=()):
        scaled = call(
            functools.partial(scale_kernel, len(ks)),
            (near_out, from_core(far_out), mix),
            [VMEM] * 3,
            [((near_out.shape[0], width), BF16)] * len(ks),
            10,
            after=after,
        )
        return scaled, {k: from_peer(p, k) for k, p in zip(ks, scaled)}

    def lay_out(ds, returned, after=()):
        return call(
            functools.partial(spread_kernel, n_exp, len(ds)),
            (*[takes[d] for d in ds], *[returned[k] for k in range(n_exp)]),
            [VMEM] * (len(ds) + n_exp),
            [((tok, width), F32 if d == 0 else BF16) for d in ds],
            10,
            after=after,
        )

    spread = [None] * n_chip
    normed_a, mix_a = take_in(groups[0], picked_all)
    act_a = run_up(normed_a)
    first_a = run_down(act_a, halves[0])
    second_a = run_down(act_a, halves[1], first_a[:1])
    normed_b, mix_b = take_in(groups[1], second_a[:1])
    scaled, returned_a = give_back(halves[0], *first_a, mix_a)
    more, rest = give_back(halves[1], *second_a, mix_a, scaled[:1])
    returned_a |= rest
    act_b = run_up(normed_b, more[:1])
    first_b = run_down(act_b, halves[0])
    waits = [returned_a[n_exp - 1]]
    second_b = run_down(act_b, halves[1], (first_b[0], *waits))
    scaled, returned_b = give_back(halves[0], *first_b, mix_b)
    more, rest = give_back(halves[1], *second_b, mix_b, scaled[:1])
    returned_b |= rest
    for d, m in zip(groups[0], lay_out(groups[0], returned_a, more[:1])):
        spread[d] = m
    for d, m in zip(groups[1], lay_out(groups[1], returned_b)):
        spread[d] = m
    total = hidden[:tok].astype(F32) + spread[0]
    for d in range(1, n_chip):
        total += from_chip(spread[d], n_chip - d).astype(F32)
    return total.astype(BF16)


def solution(mesh):
    return jax.shard_map(
        body,
        mesh=mesh,
        in_specs=(
            P("ctx", "exp"),
            P("ctx", "exp"),
            P("ctx", "exp"),
            P("ctx", "exp"),
            P(),
            P(),
            P(),
            P(("ctx", "exp"), None),
            P("exp", None, "ctx"),
            P("exp", None, "ctx"),
            P("exp", "ctx", None),
        ),
        out_specs=P("ctx", "exp"),
        check_vma=False,
    )
```

```python
import functools
import math

import jax
import jax.numpy as jnp
from jax import lax
from jax.experimental import pallas as pl
from jax.experimental.pallas import tpu as pltpu
from jax.sharding import PartitionSpec as P

HEAD_WIDTH = 128
TILE = 16
LANES = 128
F32, BF16 = jnp.float32, jnp.bfloat16
MIB = 2**20
VMEM = pl.BlockSpec(memory_space=pltpu.VMEM)
ANY = pl.BlockSpec(memory_space=pl.ANY)
SMEM = pl.BlockSpec(memory_space=pltpu.SMEM)


def call(kernel, inputs, specs, shapes, limit, scratch=(), after=(), kept=()):
    n = len(inputs)

    def ordered(*refs):
        kernel(*refs[:n], *refs[n + len(after) :])

    return pl.pallas_call(
        ordered,
        in_specs=list(specs) + [ANY] * len(after),
        out_specs=[VMEM] * (len(shapes) + len(kept)),
        out_shape=[jax.ShapeDtypeStruct(s, d) for s, d in shapes] + list(kept),
        scratch_shapes=list(scratch),
        compiler_params=pltpu.CompilerParams(vmem_limit_bytes=limit * MIB),
    )(*inputs, *after)


def pack_kernel(
    where_ref, ids_ref, k_ref, v_ref, q_ref, res_ref, w_ref,
    out_ref, row_ref, q_out, res_out, w_out, ids_vmem, sems,
):
    kv = k_ref.shape[1]
    sub = ids_ref.shape[1]
    copies = [
        pltpu.make_async_copy(ids_ref, ids_vmem, sems.at[0]),
        pltpu.make_async_copy(k_ref, out_ref.at[:, :kv], sems.at[1]),
        pltpu.make_async_copy(v_ref, out_ref.at[:, kv:], sems.at[2]),
        pltpu.make_async_copy(q_ref, q_out, sems.at[3]),
        pltpu.make_async_copy(res_ref, res_out, sems.at[4]),
        pltpu.make_async_copy(w_ref, w_out, sems.at[5]),
    ]
    for copy in copies:
        copy.start()
    copies[0].wait()
    row = lax.broadcasted_iota(jnp.int32, (TILE, sub), 0)
    two = jnp.where(row == 0, ids_vmem[0:1, :], jnp.where(row == 1, ids_vmem[1:2, :], 0))
    token = lax.broadcasted_iota(jnp.int32, (sub, LANES), 0) + where_ref[1] * sub
    lane = lax.broadcasted_iota(jnp.int32, (sub, LANES), 1)
    place = (token == lane).astype(F32)
    row_ref[...] = jnp.zeros(row_ref.shape, BF16)
    row_ref[:TILE, :LANES] = jnp.dot(
        two.astype(F32), place, preferred_element_type=F32
    ).astype(BF16)
    for copy in copies[1:]:
        copy.wait()


def join_kernel(n, *refs):
    spans, rows, (out_ref, row_ref) = refs[:n], refs[n:-2], refs[-2:]
    tok = spans[0].shape[0]
    for d in range(n):
        out_ref[d * tok : (d + 1) * tok, :] = spans[d][...]
    total = rows[0][:TILE, :LANES].astype(F32)
    for other in rows[1:]:
        total += other[:TILE, :LANES].astype(F32)
    row_ref[...] = total.astype(BF16)


def attention_kernel(n, where_ref, q_ref, res_ref, near_ref, far_ref, row_ref, hid_ref):
    tok, width = q_ref.shape
    kv = near_ref.shape[1] // 2
    heads = kv // HEAD_WIDTH
    group = width // kv
    ctx = where_ref[0]
    chip, core = ctx // 2, ctx % 2
    own = where_ref[2 + ctx] * tok
    ahead = lax.broadcasted_iota(jnp.int32, (tok, tok), 0) - lax.broadcasted_iota(
        jnp.int32, (tok, tok), 1
    )
    pieces = []
    for side in (core, 1 - core):
        for d in range(n):
            span = 2 * ((chip + d) % n) + side
            pieces.append(jnp.where(ahead >= where_ref[2 + span] * tok - own, 0.0, -1e30))
    bias = jnp.concatenate(pieces, axis=1)
    bias = jnp.concatenate([bias] * group, axis=0)
    for h in range(heads):
        cols = slice(h * HEAD_WIDTH, (h + 1) * HEAD_WIDTH)
        vals = slice(kv + h * HEAD_WIDTH, kv + (h + 1) * HEAD_WIDTH)
        key = jnp.concatenate([near_ref[:, cols], far_ref[:, cols]], axis=0)
        value = jnp.concatenate([near_ref[:, vals], far_ref[:, vals]], axis=0)
        base = h * group * HEAD_WIDTH
        q = jnp.concatenate(
            [q_ref[:, base + g * HEAD_WIDTH : base + (g + 1) * HEAD_WIDTH] for g in range(group)],
            axis=0,
        )
        s = lax.dot_general(q, key, (((1,), (1,)), ((), ())), preferred_element_type=F32)
        s = s * (1.0 / math.sqrt(HEAD_WIDTH)) + bias
        w = jnp.exp(s - jnp.max(s, axis=1, keepdims=True))
        total = jnp.sum(w, axis=1, keepdims=True)
        att = jnp.dot(w.astype(BF16), value, preferred_element_type=F32) / total
        for g in range(group):
            at = slice(base + g * HEAD_WIDTH, base + (g + 1) * HEAD_WIDTH)
            rows = att[g * tok : (g + 1) * tok]
            hid_ref[:tok, at] = (res_ref[:, at].astype(F32) + rows).astype(BF16)
    hid_ref[tok:, :] = jnp.zeros((TILE, width), BF16)
    hid_ref[tok:, :LANES] = row_ref[...]


def pick_kernel(n_exp, slots, tok, n, where_ref, *refs):
    blocks, refs = refs[:n], refs[n:]
    outs, takes, others = refs[:n_exp], refs[n_exp : n_exp + n], refs[n_exp + n :]
    exp = where_ref[1]
    earlier = (
        lax.broadcasted_iota(jnp.int32, (LANES, LANES), 0)
        < lax.broadcasted_iota(jnp.int32, (LANES, LANES), 1)
    ).astype(BF16)
    row = lax.broadcasted_iota(jnp.int32, (TILE, LANES), 0)
    lane = lax.broadcasted_iota(jnp.int32, (TILE, LANES), 1)
    slot = lax.broadcasted_iota(jnp.int32, (slots, LANES), 0).astype(F32)
    target = (exp ^ row).astype(F32)
    chosen = []
    for i in range(n):
        both = blocks[i][tok:, :LANES].astype(F32)
        first, second = both[0:1, :], both[1:2, :]
        sent = jnp.where(((first == target) | (second == target)) & (lane < tok), 1.0, 0.0)
        rank = jnp.dot(sent.astype(BF16), earlier, preferred_element_type=F32)
        chosen.append([])
        for k in range(n_exp):
            one = jnp.where(slot == rank[k : k + 1, :], sent[k : k + 1, :], 0.0)
            take = one[:, :tok].astype(BF16)
            takes[i][k] = take
            chosen[i].append(take)
            if k == 0:
                other = jnp.sum(one * (first + second), axis=1, keepdims=True) - exp.astype(F32)
                others[i][...] = jnp.broadcast_to(other, (slots, LANES))
    for k in range(n_exp):
        rows = [
            jnp.dot(chosen[i][k], blocks[i][:tok, :], preferred_element_type=F32)
            for i in range(n)
        ]
        outs[k][...] = (rows[0] if n == 1 else jnp.concatenate(rows, axis=0)).astype(BF16)


def norm_kernel(n_exp, n, parts, where_ref, gain_ref, router_ref, *refs):
    others, pieces, (out_ref, mix_ref) = refs[:n], refs[n:-2], refs[-2:]
    exp = where_ref[1]
    width = pieces[0].shape[1]
    rows = out_ref.shape[0]

    def load(k):
        held = [pieces[p * n_exp + k][...].astype(F32) for p in range(parts)]
        return held[0] if parts == 1 else jnp.concatenate(held, axis=0)

    square = jnp.zeros((rows, 1), F32)
    for k in range(n_exp):
        x = load(k)
        square += jnp.sum(x * x, axis=1, keepdims=True)
    scale = lax.rsqrt(square * (1.0 / (n_exp * width)) + 1e-05)
    logits = jnp.zeros((rows, router_ref.shape[0]), F32)
    for k in range(n_exp):
        at = pl.ds(pl.multiple_of((exp ^ k) * width, width), width)
        normed = (load(k) * scale * gain_ref[:, at].astype(F32)).astype(BF16)
        out_ref[:, at] = normed
        logits += lax.dot_general(
            normed, router_ref[:, at], (((1,), (1,)), ((), ())), preferred_element_type=F32
        )
    col = lax.broadcasted_iota(jnp.int32, logits.shape, 1)
    other = jnp.concatenate([o[...] for o in others], axis=0)[:, :1]
    own = jnp.sum(jnp.where(col == exp, logits, 0.0), axis=1, keepdims=True)
    rival = jnp.sum(jnp.where(col.astype(F32) == other, logits, 0.0), axis=1, keepdims=True)
    mix = 1.0 / (1.0 + jnp.exp(rival - own))
    mix_ref[...] = jnp.broadcast_to(mix, (rows, LANES))


def up_kernel(n, fetch, near_ref, far_ref, g_ref, u_ref, act_ref, *refs):
    kept, (x_ref, acc, sems) = refs[:-3], refs[-3:]
    held = kept if fetch else (g_ref, u_ref)
    rows = near_ref.shape[0]
    depth = held[0].shape[0] // n
    at = [slice(j * depth, (j + 1) * depth) for j in range(n)]
    copies = []
    if fetch:
        copies = [
            pltpu.make_async_copy(w.at[0, part], v.at[part], sems.at[i * n + j])
            for i, (w, v) in enumerate(((g_ref, kept[0]), (u_ref, kept[1])))
            for j, part in enumerate(at)
        ]
    for copy in copies:
        copy.start()
    x_ref[:rows, :] = near_ref[...]
    x_ref[rows:, :] = far_ref[...]
    for j in range(2 * n):
        if fetch:
            copies[j].wait()
        part = at[j % n]
        y = jnp.dot(x_ref[:, part], held[j // n][part, :], preferred_element_type=F32)
        if j % n == 0:
            acc[j // n] = y
        elif j < 2 * n - 1:
            acc[j // n] += y
        else:
            g = acc[0]
            act_ref[...] = (g * (acc[1] + y) / (1.0 + jnp.exp(-g))).astype(BF16)


def down_kernel(ks, fetch, where_ref, act_ref, d_ref, near_out, far_out, *refs):
    kept, sems = refs[:-1], refs[-1]
    held = kept[0] if fetch else d_ref
    exp = where_ref[1]
    rows = near_out.shape[0]
    width = held.shape[2]
    copies = []
    if fetch:
        for j, k in enumerate(ks):
            at = pl.ds(pl.multiple_of((exp ^ k) * width, width), width)
            copies.append(pltpu.make_async_copy(d_ref.at[0, :, at], held.at[j], sems.at[j]))
    for copy in copies:
        copy.start()
    for j in range(len(ks)):
        if fetch:
            copies[j].wait()
        y = jnp.dot(act_ref[...], held[j], preferred_element_type=F32).astype(BF16)
        near_out[:, j * width : (j + 1) * width] = y[:rows]
        far_out[:, j * width : (j + 1) * width] = y[rows:]


def scale_kernel(n, near_ref, back_ref, mix_ref, *outs):
    width = outs[0].shape[1]
    mix = mix_ref[:, :1]
    for j in range(n):
        at = slice(j * width, (j + 1) * width)
        both = near_ref[:, at].astype(F32) + back_ref[:, at].astype(F32)
        outs[j][...] = (both * mix).astype(BF16)


def spread_kernel(n_exp, n, *refs):
    takes, parts, outs = refs[:n], refs[n : n + n_exp], refs[n + n_exp :]
    slots = takes[0].shape[1]
    for i in range(n):
        total = None
        for k in range(n_exp):
            rows = parts[k][...].astype(F32)[i * slots : (i + 1) * slots].astype(BF16)
            one = lax.dot_general(
                takes[i][k], rows, (((0,), (0,)), ((), ())), preferred_element_type=F32
            )
            total = one if total is None else total + one
        outs[i][...] = total.astype(outs[i].dtype)


def body(
    queries,
    rotated_keys,
    values,
    residual,
    span_order,
    norm_gain,
    router_weight,
    expert_ids,
    gate_weight,
    up_weight,
    down_weight,
):
    tok, width = queries.shape
    n_ctx, n_exp = lax.axis_size("ctx"), lax.axis_size("exp")
    n_chip = n_ctx // 2
    kv = rotated_keys.shape[1]
    sub = tok // n_exp
    experts = n_exp * gate_weight.shape[0]
    cap = max(2, min(sub, 3 * sub // experts))
    slots = n_exp * cap
    d_model = norm_gain.shape[0]
    where = jnp.concatenate(
        [jnp.stack([lax.axis_index("ctx"), lax.axis_index("exp")]).astype(jnp.int32), span_order]
    )

    def from_chip(x, d):
        pairs = [(2 * ((i // 2 + d) % n_chip) + i % 2, i) for i in range(n_ctx)]
        return lax.ppermute(x, "ctx", pairs) if d else x

    def from_core(x):
        return lax.ppermute(x, "ctx", [(i ^ 1, i) for i in range(n_ctx)])

    def from_peer(x, k):
        return lax.ppermute(x, "exp", [(i ^ k, i) for i in range(n_exp)]) if k else x

    packed, id_row, q_near, res_near, router = call(
        pack_kernel,
        (
            where,
            *[
                pltpu.with_memory_space_constraint(x, pltpu.HBM)
                for x in (expert_ids.T, rotated_keys, values, queries, residual, router_weight.T)
            ],
        ),
        [SMEM] + [ANY] * 6,
        [((tok, 2 * kv), BF16)] * 2 + [((tok, width), BF16)] * 2
        + [((experts, d_model), BF16)],
        4,
        [pltpu.VMEM((2, sub), jnp.int32), pltpu.SemaphoreType.DMA((6,))],
    )
    near = [from_chip(packed, d) for d in range(n_chip)]
    id_rows = [from_peer(id_row, k) for k in range(n_exp)]
    joined, id_all = call(
        functools.partial(join_kernel, n_chip),
        (*near, *id_rows),
        [VMEM] * (n_chip + n_exp),
        [((n_chip * tok, 2 * kv), BF16), ((TILE, LANES), BF16)],
        4,
    )
    score_mib = 4 * width // HEAD_WIDTH * tok * n_ctx * tok // (kv // HEAD_WIDTH) // MIB
    (hidden,) = call(
        functools.partial(attention_kernel, n_chip),
        (where, q_near, res_near, joined, from_core(joined), id_all),
        [SMEM] + [VMEM] * 5,
        [((tok + TILE, width), BF16)],
        8 + 4 * score_mib,
    )
    hidden_units = gate_weight.shape[2]
    gain = norm_gain.reshape(1, d_model)

    half = n_chip // 2
    forward = list(range(half)) + list(range(n_chip - 1, half - 1, -1))
    groups = [forward[:half], forward[half:]]
    takes, others, pieces = {}, {}, {}

    def pick(ds, blocks, after=()):
        n = len(ds)
        got = call(
            functools.partial(pick_kernel, n_exp, slots, tok, n),
            (where, *blocks),
            [SMEM] + [VMEM] * n,
            [((n * slots, width), BF16)] * n_exp
            + [((n_exp, slots, tok), BF16)] * n
            + [((slots, LANES), F32)] * n,
            10,
            after=after,
        )
        for i, d in enumerate(ds):
            takes[d], others[d] = got[n_exp + i], got[n_exp + n + i]
        pieces[ds[0]] = [from_peer(got[k], k) for k in range(n_exp)]

    messages = [m for m in (groups[0][:1], groups[0][1:], groups[1]) if m]
    pick(messages[0], [hidden])
    arriving = {1: from_chip(hidden, 1)}
    for d in range(2, half):
        arriving[d] = from_chip(arriving[d - 1], 1)
    for d in range(n_chip - 1, half, -1):
        arriving[d] = from_chip(hidden if d == n_chip - 1 else arriving[d + 1], n_chip - 1)
    if half > 1:
        pick(
            messages[1],
            [arriving[d] for d in messages[1]],
            (*pieces[0][1:],),
        )
        arriving[half] = from_chip(arriving[half - 1], 1)
    pick(messages[-1], [arriving[d] for d in messages[-1]])
    picked_all = (others[messages[-1][0]],)

    def take_in(ds, after=()):
        sets = [pieces[d] for d in ds if d in pieces]
        parts = [p for part in sets for p in part]
        rows = len(ds) * slots
        return call(
            functools.partial(norm_kernel, n_exp, len(ds), len(sets)),
            (where, gain, router, *[others[d] for d in ds], *parts),
            [SMEM] + [VMEM] * (2 + len(ds) + len(parts)),
            [((rows, d_model), BF16), ((rows, LANES), F32)],
            8,
            after=after,
        )

    gate_hbm, up_hbm, down_hbm = (
        pltpu.with_memory_space_constraint(w, pltpu.HBM)
        for w in (gate_weight, up_weight, down_weight)
    )

    n_part = 4
    weights = {}

    def run_up(normed, after=()):
        rows = normed.shape[0]
        fetch = "up" not in weights
        spec = ANY if fetch else VMEM
        act, *kept = call(
            functools.partial(up_kernel, n_part, fetch),
            (normed, from_core(normed), *(weights["up"] if not fetch else (gate_hbm, up_hbm))),
            [VMEM, VMEM, spec, spec],
            [((2 * rows, hidden_units), BF16)],
            10,
            [
                pltpu.VMEM((2 * rows, d_model), BF16),
                pltpu.VMEM((2, 2 * rows, hidden_units), F32),
                pltpu.SemaphoreType.DMA((2 * n_part,)),
            ],
            after=after,
            kept=[pltpu.VMEM((d_model, hidden_units), BF16)] * (2 * fetch),
        )
        if fetch:
            weights["up"] = kept
        return act

    order = list(range(n_exp))[::-1]
    halves = [order[: n_exp // 2], order[n_exp // 2 :]]

    def run_down(act, ks, after=()):
        fetch = ks[0] not in weights
        near_out, far_out, *kept = call(
            functools.partial(down_kernel, ks, fetch),
            (where, act, down_hbm if fetch else weights[ks[0]]),
            [SMEM, VMEM, ANY if fetch else VMEM],
            [((act.shape[0] // 2, len(ks) * width), BF16)] * 2,
            6,
            [pltpu.SemaphoreType.DMA((len(ks),))],
            after=after,
            kept=[pltpu.VMEM((len(ks), hidden_units, width), BF16)] * fetch,
        )
        if fetch:
            weights[ks[0]] = kept[0]
        return near_out, far_out

    def give_back(ks, near_out, far_out, mix, after=()):
        scaled = call(
            functools.partial(scale_kernel, len(ks)),
            (near_out, from_core(far_out), mix),
            [VMEM] * 3,
            [((near_out.shape[0], width), BF16)] * len(ks),
            10,
            after=after,
        )
        return scaled, {k: from_peer(p, k) for k, p in zip(ks, scaled)}

    def lay_out(ds, returned, after=()):
        return call(
            functools.partial(spread_kernel, n_exp, len(ds)),
            (*[takes[d] for d in ds], *[returned[k] for k in range(n_exp)]),
            [VMEM] * (len(ds) + n_exp),
            [((tok, width), F32 if d == 0 else BF16) for d in ds],
            10,
            after=after,
        )

    spread = [None] * n_chip
    normed_a, mix_a = take_in(groups[0], picked_all)
    act_a = run_up(normed_a)
    first_a = run_down(act_a, halves[0])
    second_a = run_down(act_a, halves[1], first_a[:1])
    normed_b, mix_b = take_in(groups[1], second_a[:1])
    scaled, returned_a = give_back(halves[0], *first_a, mix_a)
    more, rest = give_back(halves[1], *second_a, mix_a, scaled[:1])
    returned_a |= rest
    act_b = run_up(normed_b, more[:1])
    first_b = run_down(act_b, halves[0])
    waits = [returned_a[n_exp - 1]]
    second_b = run_down(act_b, halves[1], (first_b[0], *waits))
    scaled, returned_b = give_back(halves[0], *first_b, mix_b)
    more, rest = give_back(halves[1], *second_b, mix_b, scaled[:1])
    returned_b |= rest
    for d, m in zip(groups[0], lay_out(groups[0], returned_a, more[:1])):
        spread[d] = m
    for d, m in zip(groups[1], lay_out(groups[1], returned_b)):
        spread[d] = m
    total = hidden[:tok].astype(F32) + spread[0]
    for d in range(1, n_chip):
        total += from_chip(spread[d], n_chip - d).astype(F32)
    return total.astype(BF16)


def solution(mesh):
    return jax.shard_map(
        body,
        mesh=mesh,
        in_specs=(
            P("ctx", "exp"),
            P("ctx", "exp"),
            P("ctx", "exp"),
            P("ctx", "exp"),
            P(),
            P(),
            P(),
            P(("ctx", "exp"), None),
            P("exp", None, "ctx"),
            P("exp", None, "ctx"),
            P("exp", "ctx", None),
        ),
        out_specs=P("ctx", "exp"),
        check_vma=False,
    )
```
